32 devices in a mesh: ctx: 8 (over y, x, core), head: 4 (over z).
Axes of the slice: x: 2, y: 2, z: 4, core: 2. Of those that a mesh axis runs over, the one named last changes fastest.
Arguments:
- queries: bfloat16 [32, 16384, 128], P('head', 'ctx'), may hold values from -6 to 6
- key_states: bfloat16 [16, 16384, 128], P('head', 'ctx'), may hold values from -6 to 6
- value_states: bfloat16 [16, 16384, 128], P('head', 'ctx'), may hold values from -6 to 6
- attn_output: bfloat16 [16384, 4096], P(('ctx', 'head')), may hold values from -6 to 6
- out_cotangent: bfloat16 [16384, 4096], P(('ctx', 'head')), may hold values from -6 to 6
- logsumexp: float32 [32, 16384], P('head', 'ctx'), may hold values from 4.5 to 6.5
- doc_start: int32 [16384], P('ctx'), may hold values from 0 to 15360, as said below
Outputs:
- grad_queries: bfloat16 [32, 16384, 128], P('head', 'ctx')
- grad_keys: bfloat16 [16, 16384, 128], P('head', 'ctx')
- grad_values: bfloat16 [16, 16384, 128], P('head', 'ctx')
The draws below stay inside these ranges and needn't reach their ends.
Inputs may be any that keep to these rules, and one draw needn't show every extreme that they name: doc_start[t] <= t and never falls; each value is the first position of a document; doc_start[0] = 0; the last 1024 positions form one document that starts at 15360; every other document has half of 1024 to 3072 tokens, except that the one just before the last may be shorter.
All inputs are finite; a program needn't handle non-finite values.
Results may differ from the reference program's by a relative error of at most 0.0049.
Values may be sent and summed in bfloat16 or wider, within the bound.
No kernel may reach another device: no remote copies, remote signals or barrier semaphores. Data moves between devices by JAX's collectives and lax.ppermute only.
A program may use at most 192 MiB of HBM per device.

```python
import jax
import jax.numpy as jnp
from jax import lax

HQ = 32
KV = 16
HD = 128
W = 1024
QPRE = 168
TOK_DEV = 2048
TOKENS = 16384


def draw_doc_start(key, part):
    lowest = max(W // 2, 1)
    highest = 3 * W + 1
    doc_count = TOKENS // lowest + 2
    lengths = jax.random.randint(key, (doc_count,), lowest, highest, dtype=jnp.int32)
    doc_ends = jnp.cumsum(lengths).astype(jnp.int32)
    starts = jnp.concatenate([jnp.zeros((1,), jnp.int32), doc_ends[:-1]])
    positions = jnp.arange(TOKENS, dtype=jnp.int32)
    owner_index = (jnp.searchsorted(starts, positions, side='right') - 1).astype(jnp.int32)
    drawn = starts[owner_index].astype(jnp.int32)
    last_start = jnp.int32(TOKENS - W)
    return jnp.where(positions >= last_start, last_start, drawn).astype(jnp.int32)


def block_levels(rng, dims, split, low, high):
    factor_of = 1.0
    for dim, blocks in split:
        steps = jax.random.uniform(jax.random.fold_in(jax.random.fold_in(rng, 6), dim), (blocks,), jnp.float32, low / len(split), high / len(split))
        factor_of = factor_of * jnp.repeat(jnp.exp(steps), dims[dim] // blocks).reshape((-1,) + (1,) * (len(dims) - 1 - dim))
    return factor_of


def gaussian(rng, shape, deviation, most, cuts=(), kind=jnp.bfloat16):
    factor_of = block_levels(rng, shape, cuts, -0.22, 0.18) if cuts else 1.0
    array = jax.random.normal(rng, shape, jnp.float32) * deviation * factor_of
    return jnp.minimum(jnp.maximum(array, -most), most).astype(kind)


def setup_inputs(seed: int = 0) -> dict:
    key_list = jax.random.split(jax.random.key(seed), 8)
    queries = gaussian(key_list[0], (HQ, TOKENS, HD), 1.0, 6.0, ((0, 4), (1, 8)))
    key_states = gaussian(key_list[1], (KV, TOKENS, HD), 1.0, 6.0, ((0, 4), (1, 8)))
    value_states = gaussian(key_list[2], (KV, TOKENS, HD), 1.0, 6.0, ((0, 4), (1, 8)))
    attn_output = gaussian(key_list[3], (TOKENS, HQ * HD), 1.0, 6.0, ((0, 32),))
    out_cotangent = gaussian(key_list[4], (TOKENS, HQ * HD), 1.0, 6.0, ((0, 32),))
    logsumexp = jnp.clip(4.5 + 2.0 * jax.random.uniform(key_list[5], (HQ, TOKENS), jnp.float32) ** block_levels(key_list[5], (HQ, TOKENS), ((0, 4), (1, 8)), -0.2, 0.2), 4.5, 6.5)
    doc_start = draw_doc_start(jax.random.fold_in(key_list[7], 71), 0)
    return {"queries": queries, "key_states": key_states, "value_states": value_states, "attn_output": attn_output, "out_cotangent": out_cotangent, "logsumexp": logsumexp, "doc_start": doc_start}


def band_tile(query_block, cotan_block, lse_block, delta_block, key_block, value_block, allowed, score_scale):
    f32 = jnp.float32
    scores = jnp.einsum("kgrd,kjd->kgrj", query_block.astype(f32), key_block.astype(f32)) * score_scale
    probs = jnp.where(allowed, jnp.exp(scores - lse_block[..., None]), jnp.float32(0.0))
    probs_low = probs.astype(jnp.bfloat16)
    dprobs = jnp.einsum("rkgd,kjd->kgrj", cotan_block.astype(f32), value_block.astype(f32))
    dscores = (probs * (dprobs - delta_block[..., None])).astype(jnp.bfloat16)
    grad_value = jnp.einsum("kgrj,rkgd->kjd", probs_low.astype(f32), cotan_block.astype(f32))
    grad_key = jnp.einsum("kgrj,kgrd->kjd", dscores.astype(f32), query_block.astype(f32)) * score_scale
    grad_query = jnp.einsum("kgrj,kjd->kgrd", dscores.astype(f32), key_block.astype(f32)) * score_scale
    return grad_query, grad_key, grad_value


def reference(queries, key_states, value_states, attn_output, out_cotangent, logsumexp, doc_start):
    kv_heads = key_states.shape[0]
    total = key_states.shape[1]
    head_dim = key_states.shape[2]
    groups = HQ // KV
    window = W
    block_rows = min(512, TOK_DEV)
    n_blocks = total // block_rows
    span = block_rows + window
    score_scale = QPRE ** -0.5
    cotangent = out_cotangent.reshape(total, HQ, head_dim)
    output = attn_output.reshape(total, HQ, head_dim)
    row_delta = jnp.sum(cotangent.astype(jnp.float32) * output.astype(jnp.float32), axis=2)
    delta_grouped = row_delta.reshape(total, kv_heads, groups).transpose(1, 2, 0)
    lse_grouped = logsumexp.reshape(kv_heads, groups, total)
    query_grouped = queries.reshape(kv_heads, groups, total, head_dim)
    padding = jnp.zeros((kv_heads, window, head_dim), jnp.bfloat16)
    key_ext = jnp.concatenate([padding, key_states], axis=1)
    value_ext = jnp.concatenate([padding, value_states], axis=1)
    row_iota = jnp.arange(block_rows, dtype=jnp.int32)
    col_iota = jnp.arange(span, dtype=jnp.int32)
    distance = row_iota[:, None] + window - col_iota[None, :]
    near = (distance >= 0) & (distance < window)

    def block_step(index, carry):
        grad_key_ext, grad_value_ext, grad_query_all = carry
        first = (index * block_rows).astype(jnp.int32)
        query_block = lax.dynamic_slice_in_dim(query_grouped, first, block_rows, 2)
        lse_block = lax.dynamic_slice_in_dim(lse_grouped, first, block_rows, 2)
        delta_block = lax.dynamic_slice_in_dim(delta_grouped, first, block_rows, 2)
        cotan_block = lax.dynamic_slice_in_dim(cotangent, first, block_rows, 0).reshape(block_rows, kv_heads, groups, head_dim)
        key_block = lax.dynamic_slice_in_dim(key_ext, first, span, 1)
        value_block = lax.dynamic_slice_in_dim(value_ext, first, span, 1)
        start_rel = lax.dynamic_slice_in_dim(doc_start, first, block_rows, 0)
        key_local = first - window + col_iota
        allowed = near & (key_local[None, :] >= start_rel[:, None])
        grad_query, grad_key, grad_value = band_tile(query_block, cotan_block, lse_block, delta_block, key_block, value_block, allowed, score_scale)
        grad_key_ext = lax.dynamic_update_slice_in_dim(grad_key_ext, lax.dynamic_slice_in_dim(grad_key_ext, first, span, 1) + grad_key, first, 1)
        grad_value_ext = lax.dynamic_update_slice_in_dim(grad_value_ext, lax.dynamic_slice_in_dim(grad_value_ext, first, span, 1) + grad_value, first, 1)
        grad_query_all = lax.dynamic_update_slice_in_dim(grad_query_all, grad_query.astype(jnp.bfloat16), first, 2)
        return grad_key_ext, grad_value_ext, grad_query_all

    initial = (jnp.zeros((kv_heads, total + window, head_dim), jnp.float32),
               jnp.zeros((kv_heads, total + window, head_dim), jnp.float32),
               jnp.zeros((kv_heads, groups, total, head_dim), jnp.bfloat16))
    grad_key_ext, grad_value_ext, grad_query_all = lax.fori_loop(0, n_blocks, block_step, initial)
    grad_queries = grad_query_all.reshape(HQ, total, head_dim)
    grad_keys = grad_key_ext[:, window:].astype(jnp.bfloat16)
    grad_values = grad_value_ext[:, window:].astype(jnp.bfloat16)
    return (grad_queries, grad_keys, grad_values)
```

```python
import functools
import math

import jax
import jax.numpy as jnp
from jax import lax
from jax.experimental import pallas as pl
from jax.experimental.pallas import tpu as pltpu
from jax.sharding import PartitionSpec as P

W = 1024
QPRE = 168
BLOCK = 128
LOG2E = math.log2(math.e)
F32 = jnp.float32
BF16 = jnp.bfloat16
NT = (((1,), (1,)), ((), ()))
NN = (((1,), (0,)), ((), ()))


def from_behind(block, axis, distance):
    devices = range(lax.axis_size(axis))
    route = [(i - distance, i) for i in devices if i - distance in devices]
    return lax.ppermute(block, axis, route)


def delta_kernel(cotan_ref, output_ref, delta_ref):
    rows, width = cotan_ref.shape
    heads = delta_ref.shape[0]
    product = cotan_ref[...].astype(F32) * output_ref[...].astype(F32)
    high = product.astype(BF16)
    low = (product - high.astype(F32)).astype(BF16)
    head_of = lax.broadcasted_iota(jnp.int32, (heads, width), 1) // (width // heads)
    member = (head_of == lax.broadcasted_iota(jnp.int32, (heads, width), 0)).astype(BF16)
    total = lax.dot_general(member, high, NT, preferred_element_type=F32)
    delta_ref[...] = total + lax.dot_general(member, low, NT, preferred_element_type=F32)


def row_deltas(cotan, output, heads):
    rows, width = cotan.shape
    step = min(128, rows)
    return pl.pallas_call(
        delta_kernel,
        grid=(rows // step,),
        in_specs=[pl.BlockSpec((step, width), lambda i: (i, 0))] * 2,
        out_specs=pl.BlockSpec((heads, step), lambda i: (0, i)),
        out_shape=jax.ShapeDtypeStruct((heads, rows), F32),
        cost_estimate=pl.CostEstimate(
            flops=4 * rows * width * heads, bytes_accessed=4 * rows * width, transcendentals=0
        ),
        name="row_deltas",
    )(cotan, output)


def head_kernel(head, pieces, aliased, me_ref, *refs):
    refs = list(refs)
    q_ref, kh_ref, ko_ref, vh_ref, vo_ref, lse_ref, start_ref = refs[:7]
    cotan_refs = refs[7 : 7 + pieces]
    delta_refs = refs[7 + pieces : 7 + 2 * pieces]
    rest = refs[7 + 2 * pieces + aliased :]
    dq_ref, dk_ref, dv_ref, dk_tail_ref, dv_tail_ref, halo_ref = rest[:6]
    k_all, v_all, kt_all, dk_all, dv_all, ds_all = rest[6:]
    step = pl.program_id(0)
    steps = pl.num_programs(0)
    window = kh_ref.shape[1]
    groups = q_ref.shape[0]
    span = window + BLOCK
    cols = groups * BLOCK
    scale = QPRE ** (-0.5)

    @pl.when(step == 0)
    def _():
        k_all[:window] = kh_ref[0]
        k_all[window:] = ko_ref[0]
        v_all[:window] = vh_ref[0]
        v_all[window:] = vo_ref[0]
        for i in range(k_all.shape[0] // BLOCK):
            rows = pl.ds(i * BLOCK, BLOCK)
            kt_all[:, rows] = k_all[rows, :].T
        dk_all[...] = jnp.zeros_like(dk_all)
        dv_all[...] = jnp.zeros_like(dv_all)

    first = pl.multiple_of(step * BLOCK, BLOCK)
    piece_rows = steps * BLOCK // pieces
    source = lax.rem(me_ref[0] - first // piece_rows + pieces, pieces)

    def pick(options):
        got = options[0]
        for i in range(1, pieces):
            got = jnp.where(source == i, options[i], got)
        return got

    def row_of(block):
        return jnp.concatenate([block[groups * head + i][None] for i in range(groups)], axis=1)

    query = q_ref[...].reshape(cols, q_ref.shape[2])
    cotan = pick([r[...] for r in cotan_refs])
    width = cotan.shape[1] // groups
    cotan = jnp.concatenate([cotan[:, i * width : (i + 1) * width] for i in range(groups)], axis=0)
    delta = row_of(pick([r[...] for r in delta_refs]))
    lse = row_of(lse_ref[...]) * F32(LOG2E)
    start = jnp.concatenate([start_ref[...]] * groups, axis=1) - first
    place = lax.broadcasted_iota(jnp.int32, (BLOCK, cols), 0)
    token = lax.broadcasted_iota(jnp.int32, (BLOCK, cols), 1) % BLOCK

    for i in range(span // BLOCK):
        rows = pl.ds(pl.multiple_of(first + i * BLOCK, BLOCK), BLOCK)
        scores = lax.dot_general(k_all[rows, :], query, NT, preferred_element_type=F32)
        dprobs = lax.dot_general(v_all[rows, :], cotan, NT, preferred_element_type=F32)
        allowed = place >= start - i * BLOCK
        if i == 0:
            allowed = allowed & (place > token)
        if i == span // BLOCK - 1:
            allowed = allowed & (place <= token)
        probs = jnp.where(allowed, jnp.exp2(scores * F32(scale * LOG2E) - lse), F32(0.0))
        dscores = (probs * (dprobs - delta)).astype(BF16)
        ds_all[i * BLOCK : (i + 1) * BLOCK, :] = dscores
        dv_all[rows, :] += lax.dot_general(probs.astype(BF16), cotan, NN, preferred_element_type=F32)
        dk_all[rows, :] += lax.dot_general(dscores, query, NN, preferred_element_type=F32)
    dq = lax.dot_general(
        kt_all[:, pl.ds(first, span)], ds_all[...], NN, preferred_element_type=F32
    )
    dq_ref[...] = (dq.T * F32(scale)).astype(BF16).reshape(dq_ref.shape)

    @pl.when(step == steps - 1)
    def _():
        own = dk_ref.shape[1]
        halo_ref[0] = (dk_all[:window] * F32(scale)).astype(BF16)
        halo_ref[1] = dv_all[:window].astype(BF16)
        dk_ref[0] = (dk_all[window : window + own] * F32(scale)).astype(BF16)
        dv_ref[0] = dv_all[window : window + own].astype(BF16)
        dk_tail_ref[...] = dk_all[window + own :] * F32(scale)
        dv_tail_ref[...] = dv_all[window + own :]


def head_call(head, me, queries, key_rim, keys, value_rim, values, lse, start, cotans, deltas, before):
    kv_heads, tok_rows, head_dim = keys.shape
    q_heads = queries.shape[0]
    groups = q_heads // kv_heads
    window = key_rim.shape[1]
    pieces = len(cotans)
    steps = tok_rows // BLOCK
    in_piece = steps // pieces
    own = tok_rows - window
    cols = groups * head_dim
    ext = tok_rows + window
    whole = pl.BlockSpec((1, tok_rows, head_dim), lambda i, me: (head, 0, 0))
    rim = pl.BlockSpec((1, window, head_dim), lambda i, me: (head, 0, 0))
    in_specs = [
        pl.BlockSpec((groups, BLOCK, head_dim), lambda i, me: (head, i, 0)),
        rim,
        whole,
        rim,
        whole,
        pl.BlockSpec((q_heads, BLOCK), lambda i, me: (0, i)),
        pl.BlockSpec((1, BLOCK), lambda i, me: (0, i)),
    ]
    in_specs += [pl.BlockSpec((BLOCK, cols), lambda i, me: (lax.rem(i, in_piece), 0))] * pieces
    in_specs += [pl.BlockSpec((q_heads, BLOCK), lambda i, me: (0, lax.rem(i, in_piece)))] * pieces
    in_specs += [pl.BlockSpec(memory_space=pl.ANY)] * len(before)
    n_in = 1 + 7 + 2 * pieces
    out_specs = [
        pl.BlockSpec((groups, BLOCK, head_dim), lambda i, me: (head, i, 0)),
        pl.BlockSpec((1, own, head_dim), lambda i, me: (head, 0, 0)),
        pl.BlockSpec((1, own, head_dim), lambda i, me: (head, 0, 0)),
        pl.BlockSpec((window, head_dim), lambda i, me: (0, 0)),
        pl.BlockSpec((window, head_dim), lambda i, me: (0, 0)),
        pl.BlockSpec((2, window, head_dim), lambda i, me: (0, 0, 0)),
    ]
    out_shape = [
        jax.ShapeDtypeStruct(queries.shape, BF16),
        jax.ShapeDtypeStruct(keys.shape, BF16),
        jax.ShapeDtypeStruct(keys.shape, BF16),
        jax.ShapeDtypeStruct((window, head_dim), F32),
        jax.ShapeDtypeStruct((window, head_dim), F32),
        jax.ShapeDtypeStruct((2, window, head_dim), BF16),
    ]
    pairs = groups * tok_rows * (window + BLOCK)
    return pl.pallas_call(
        functools.partial(head_kernel, head, pieces, len(before)),
        grid_spec=pltpu.PrefetchScalarGridSpec(
            num_scalar_prefetch=1,
            grid=(steps,),
            in_specs=in_specs,
            out_specs=out_specs,
            scratch_shapes=[
                pltpu.VMEM((ext, head_dim), BF16),
                pltpu.VMEM((ext, head_dim), BF16),
                pltpu.VMEM((head_dim, ext), BF16),
                pltpu.VMEM((ext, head_dim), F32),
                pltpu.VMEM((ext, head_dim), F32),
                pltpu.VMEM((window + BLOCK, groups * BLOCK), BF16),
            ],
        ),
        out_shape=out_shape,
        input_output_aliases={n_in + i: i for i in range(len(before))},
        compiler_params=pltpu.CompilerParams(vmem_limit_bytes=40 * 1024 * 1024),
        cost_estimate=pl.CostEstimate(
            flops=10 * pairs * head_dim * 2, bytes_accessed=8 * tok_rows * head_dim * 2, transcendentals=pairs
        ),
        name="head_backward",
    )(me, queries, key_rim, keys, value_rim, values, lse, start, *cotans, *deltas, *before)


def join_kernel(dk_tail_ref, dv_tail_ref, back_ref, dk_in, dv_in, dk_ref, dv_ref):
    dk_ref[0] = (dk_tail_ref[...] + back_ref[0].astype(F32)).astype(BF16)
    dv_ref[0] = (dv_tail_ref[...] + back_ref[1].astype(F32)).astype(BF16)


def join_call(head, dk_tail, dv_tail, back, grad_keys, grad_values):
    window, head_dim = dk_tail.shape
    last = grad_keys.shape[1] // window - 1
    tail = pl.BlockSpec((window, head_dim), lambda i: (0, 0))
    out = pl.BlockSpec((1, window, head_dim), lambda i: (head, last, 0))
    return pl.pallas_call(
        join_kernel,
        grid=(1,),
        in_specs=[
            tail,
            tail,
            pl.BlockSpec((2, window, head_dim), lambda i: (0, 0, 0)),
            pl.BlockSpec(memory_space=pl.ANY),
            pl.BlockSpec(memory_space=pl.ANY),
        ],
        out_specs=[out, out],
        out_shape=[jax.ShapeDtypeStruct(grad_keys.shape, BF16)] * 2,
        input_output_aliases={3: 0, 4: 1},
        name="join_tail",
    )(dk_tail, dv_tail, back, grad_keys, grad_values)


def body(queries, key_states, value_states, attn_output, out_cotangent, logsumexp, doc_start):
    kv_heads, tok_rows, head_dim = key_states.shape
    q_heads = queries.shape[0]
    groups = q_heads // kv_heads
    window = W
    pieces = lax.axis_size("head")
    me = lax.axis_index("head")
    total_heads = out_cotangent.shape[1] // head_dim
    width = q_heads * head_dim
    cols = groups * head_dim

    def sent(block, distance):
        route = [(i, (i + distance) % pieces) for i in range(pieces)]
        return lax.ppermute(block, "head", route)

    cotans = []
    for head in range(kv_heads):
        parts = []
        for k in range(pieces):
            target = lax.rem(me + k, pieces)
            part = lax.dynamic_slice_in_dim(out_cotangent, target * width + head * cols, cols, 1)
            parts.append(part if k == 0 else sent(part, k))
        cotans.append(parts)
    deltas_here = row_deltas(out_cotangent, attn_output, total_heads)
    deltas = []
    for k in range(pieces):
        target = lax.rem(me + k, pieces)
        part = lax.dynamic_slice_in_dim(deltas_here, target * q_heads, q_heads, 0)
        deltas.append(part if k == 0 else sent(part, k))
    key_rim, value_rim = from_behind(
        (key_states[:, tok_rows - window :], value_states[:, tok_rows - window :]), "ctx", 1
    )
    start = doc_start[None, :] - lax.axis_index("ctx") * tok_rows + window
    me_array = me.astype(jnp.int32)[None]

    before = []
    tails = []
    for head in range(kv_heads):
        got = head_call(
            head, me_array, queries, key_rim, key_states, value_rim, value_states,
            logsumexp, start, cotans[head], deltas, before,
        )
        before = list(got[:3])
        tails.append((got[3], got[4], from_behind(got[5], "ctx", -1)))
    grad_queries, grad_keys, grad_values = before
    for head in range(kv_heads):
        grad_keys, grad_values = join_call(head, *tails[head], grad_keys, grad_values)
    return (grad_queries, grad_keys, grad_values)


def solution(mesh):
    return jax.shard_map(
        body,
        mesh=mesh,
        in_specs=(
            P("head", "ctx", None),
            P("head", "ctx", None),
            P("head", "ctx", None),
            P(("ctx", "head"), None),
            P(("ctx", "head"), None),
            P("head", "ctx"),
            P("ctx"),
        ),
        out_specs=(P("head", "ctx", None), P("head", "ctx", None), P("head", "ctx", None)),
        check_vma=False,
    )
```

```python
import functools
import math

import jax
import jax.numpy as jnp
from jax import lax
from jax.experimental import pallas as pl
from jax.experimental.pallas import tpu as pltpu
from jax.sharding import PartitionSpec as P

W = 1024
QPRE = 168
BLOCK = 128
SUB = 32
UNROLL = 4
VMEM_LIMIT = 56 * 1024 * 1024
LOG2E = math.log2(math.e)
F32 = jnp.float32
BF16 = jnp.bfloat16
NT = (((1,), (1,)), ((), ()))
NN = (((1,), (0,)), ((), ()))


def from_behind(block, axis, distance):
    devices = range(lax.axis_size(axis))
    route = [(i - distance, i) for i in devices if i - distance in devices]
    return lax.ppermute(block, axis, route)


def pack_kernel(pieces, me_ref, *refs):
    cotan_refs, output_refs = refs[:pieces], refs[pieces : 2 * pieces]
    out_refs, rows_ref = refs[2 * pieces + 1 : 3 * pieces + 1], refs[3 * pieces + 1]
    rows, cols = cotan_refs[0].shape
    groups = cols // BLOCK
    in_piece = rows // BLOCK
    head_of = lax.broadcasted_iota(jnp.int32, (16, cols), 1) // BLOCK
    member = (head_of == lax.broadcasted_iota(jnp.int32, (16, cols), 0)).astype(BF16)
    rows_ref[...] = jnp.zeros_like(rows_ref)
    for k in range(pieces):
        cotan = cotan_refs[k][...]
        product = cotan.astype(F32) * output_refs[k][...].astype(F32)
        high = product.astype(BF16)
        low = (product - high.astype(F32)).astype(BF16)
        delta = lax.dot_general(member, high, NT, preferred_element_type=F32)
        delta = delta + lax.dot_general(member, low, NT, preferred_element_type=F32)
        out_refs[k][:rows] = cotan
        for part in range(3):
            rounded = delta.astype(BF16).astype(F32)
            delta = delta - rounded
            for j in range(in_piece):
                for i in range(groups):
                    rows_ref[
                        part * in_piece + j : part * in_piece + j + 1, i * BLOCK : (i + 1) * BLOCK
                    ] = rounded[i : i + 1, j * BLOCK : (j + 1) * BLOCK]
        out_refs[k][rows:] = rows_ref[...].astype(BF16)


def pack_call(head, me, cotan, output, kv_heads, cols, pieces, after):
    rows = cotan.shape[0]
    assert 3 * (rows // BLOCK) <= 16

    def piece_at(k):
        return pl.BlockSpec(
            (rows, cols), lambda i, me: (0, lax.rem(me[0] + k, pieces) * kv_heads + head)
        )

    in_specs = [piece_at(k) for k in range(pieces)] * 2 + [pl.BlockSpec(memory_space=pl.ANY)]
    operands = [cotan] * pieces + [output] * pieces + [after]
    out_specs = [pl.BlockSpec((rows + 16, cols), lambda i, me: (0, 0))] * pieces
    out_shape = [jax.ShapeDtypeStruct((rows + 16, cols), BF16)] * pieces
    scratch = [pltpu.VMEM((16, cols), F32)]
    return pl.pallas_call(
        functools.partial(pack_kernel, pieces),
        grid_spec=pltpu.PrefetchScalarGridSpec(
            num_scalar_prefetch=1,
            grid=(1,),
            in_specs=in_specs,
            out_specs=out_specs,
            scratch_shapes=scratch,
        ),
        out_shape=out_shape,
        compiler_params=pltpu.CompilerParams(vmem_limit_bytes=VMEM_LIMIT),
        cost_estimate=pl.CostEstimate(
            flops=4 * rows * cols * pieces, bytes_accessed=6 * rows * cols * pieces, transcendentals=0
        ),
        name="pack_cotangent",
    )(me, *operands)


def rim_kernel(key_ref, value_ref, after_ref, out_ref):
    out_ref[0] = key_ref[...]
    out_ref[1] = value_ref[...]


def rim_call(keys, values, after):
    kv_heads, tok_rows, head_dim = keys.shape
    last = pl.BlockSpec((1, W, head_dim), lambda i: (i, tok_rows // W - 1, 0))
    return pl.pallas_call(
        rim_kernel,
        grid=(kv_heads,),
        in_specs=[last, last, pl.BlockSpec(memory_space=pl.ANY)],
        out_specs=pl.BlockSpec((2, 1, W, head_dim), lambda i: (0, i, 0, 0)),
        out_shape=jax.ShapeDtypeStruct((2, kv_heads, W, head_dim), BF16),
        name="rims",
    )(keys, values, after)


def head_kernel(head, blocks, carried, closing, aliased, passed, me_ref, *refs):
    refs = list(refs)
    q_ref, kh_ref, ko_ref, vh_ref, vo_ref, lse_ref, start_ref = refs[:7]
    pieces = len(refs) - 7 - 2 * carried - aliased - 2 * passed - (14 if closing else 9)
    cotan_refs = refs[7 : 7 + pieces]
    refs = refs[7 + pieces :]
    dk_in, dv_in = refs[:2] if carried else (None, None)
    refs = refs[2 * carried + aliased + passed :]
    if closing:
        dq_ref, dk_ref, dv_ref, dk_tail_ref, dv_tail_ref, halo_ref = refs[:6]
        k_all, v_all, kt_all, cotan_all, delta_all, ds_all, dk_all, dv_all = refs[6 + passed :]
    else:
        dq_ref, dk_all, dv_all = refs[:3]
        k_all, v_all, kt_all, cotan_all, delta_all, ds_all = refs[3 + passed :]
    window, head_dim = kh_ref.shape[1:]
    groups, tok_rows = q_ref.shape[:2]
    piece_rows = tok_rows // pieces
    in_piece = piece_rows // BLOCK
    span = window + BLOCK
    cols = groups * BLOCK
    scale = QPRE ** (-0.5)
    me = me_ref[0]

    k_all[:window] = kh_ref[0]
    k_all[window:] = ko_ref[0]
    v_all[:window] = vh_ref[0]
    v_all[window:] = vo_ref[0]
    unit = (
        lax.broadcasted_iota(jnp.int32, (head_dim, head_dim), 0)
        == lax.broadcasted_iota(jnp.int32, (head_dim, head_dim), 1)
    ).astype(BF16)
    kt_all[...] = lax.dot_general(unit, k_all[...], NT, preferred_element_type=F32).astype(BF16)
    if carried:
        dk_all[...] = dk_in[...]
        dv_all[...] = dv_in[...]
    else:
        dk_all[...] = jnp.zeros_like(dk_all)
        dv_all[...] = jnp.zeros_like(dv_all)
    ds_all[...] = jnp.zeros_like(ds_all)
    for i in range(pieces):
        source = lax.rem(me - i + pieces, pieces)
        where = pl.ds(pl.multiple_of(source * piece_rows, piece_rows), piece_rows)
        for j in range(groups):
            cotan_all[j, where, :] = cotan_refs[i][:piece_rows, j * head_dim : (j + 1) * head_dim]
        parts = cotan_refs[i][piece_rows:].astype(F32)
        for j in range(in_piece):
            row = parts[j : j + 1] + parts[in_piece + j : in_piece + j + 1]
            delta_all[source * in_piece + j] = row + parts[2 * in_piece + j : 2 * in_piece + j + 1]

    def write_query(first, slot):
        dq = lax.dot_general(
            kt_all[:, pl.ds(first, span)], ds_all[slot], NN, preferred_element_type=F32
        )
        dq = (dq.T * F32(scale)).astype(BF16)
        into = pl.multiple_of(first - first_block * BLOCK, BLOCK)
        dq_ref[:, pl.ds(into, BLOCK), :] = dq.reshape(groups, BLOCK, head_dim)

    token = lax.broadcasted_iota(jnp.int32, (1, cols), 1) % BLOCK
    place = lax.broadcasted_iota(jnp.int32, (SUB, cols), 0)
    chunks = span // BLOCK
    first_block, count = blocks
    unroll = ds_all.shape[0]

    def load(index):
        first = pl.multiple_of(index * BLOCK, BLOCK)
        here = pl.ds(first, BLOCK)
        query = q_ref[:, here, :].reshape(cols, head_dim)
        cotan = cotan_all[:, here, :].reshape(cols, head_dim)

        rows = [lse_ref[head * groups + i : head * groups + i + 1, here] for i in range(groups)]
        lse = jnp.concatenate(rows, axis=1) * F32(LOG2E)
        delta = delta_all[index]
        start = jnp.concatenate([start_ref[:, here]] * groups, axis=1) - first
        lower = jnp.maximum(start, token + 1)
        return first, query, cotan, lse, delta, lower

    def span_of(first, i):
        return pl.ds(pl.multiple_of(first + i * BLOCK, BLOCK), BLOCK)

    def front(block, i):
        first, query, cotan = block[:3]
        rows = span_of(first, i)
        return (
            lax.dot_general(k_all[rows, :], query, NT, preferred_element_type=F32),
            lax.dot_general(v_all[rows, :], cotan, NT, preferred_element_type=F32),
        )

    def back(block, i, probs_low, dscores):
        first, query, cotan = block[:3]
        rows = span_of(first, i)
        dv_all[rows, :] += lax.dot_general(probs_low, cotan, NN, preferred_element_type=F32)
        dk_all[rows, :] += lax.dot_general(dscores, query, NN, preferred_element_type=F32)

    def middle(block, slot, i, scores, dprobs):
        _, _, _, lse, delta, lower = block
        lows = []
        for at in range(0, BLOCK, SUB):
            part = slice(at, at + SUB)
            shift = i * BLOCK + at
            allowed = place >= lower - shift
            if shift + SUB > window:
                allowed = allowed & (place <= token + (window - shift))
            probs = jnp.where(
                allowed, jnp.exp2(scores[part] * F32(scale * LOG2E) - lse), F32(0.0)
            )
            dscores = (probs * (dprobs[part] - delta)).astype(BF16)
            ds_all[slot, shift : shift + SUB, :] = dscores
            lows.append((probs.astype(BF16), dscores))
        probs_low = jnp.concatenate([x for x, _ in lows], axis=0)
        dscores = jnp.concatenate([x for _, x in lows], axis=0)
        return probs_low, dscores

    def some_blocks(index, nothing):
        blocks = [load(first_block + unroll * index + j) for j in range(unroll)]
        stages = [(j, i) for j in range(unroll) for i in range(chunks)]
        ready = front(blocks[0], 0)
        before = first_block + jnp.maximum(unroll * index - 1, 0)
        write_query(pl.multiple_of(before * BLOCK, BLOCK), unroll - 1)
        held = None
        for n, (j, i) in enumerate(stages):
            scores, dprobs = ready
            if n + 1 < len(stages):
                jj, ii = stages[n + 1]
                ready = front(blocks[jj], ii)
            if held is not None:
                back(*held)
            if i == 1 and j > 0:
                write_query(blocks[j - 1][0], j - 1)
            held = (blocks[j], i, *middle(blocks[j], j, i, scores, dprobs))
        back(*held)
        return nothing

    lax.fori_loop(0, count // unroll, some_blocks, 0)
    write_query((first_block + count - 1) * BLOCK, unroll - 1)

    if closing:
        own = dk_ref.shape[1]
        halo_ref[0] = (dk_all[:window] * F32(scale)).astype(BF16)
        halo_ref[1] = dv_all[:window].astype(BF16)
        dk_ref[0] = (dk_all[window : window + own] * F32(scale)).astype(BF16)
        dv_ref[0] = dv_all[window : window + own].astype(BF16)
        dk_tail_ref[...] = dk_all[window + own :] * F32(scale)
        dv_tail_ref[...] = dv_all[window + own :]


def head_call(
    head, blocks, me, queries, rims, keys, values, lse, start, cotans, before, carry, closing, passing
):
    kv_heads, tok_rows, head_dim = keys.shape
    q_heads = queries.shape[0]
    groups = q_heads // kv_heads
    window = rims.shape[2]
    pieces = len(cotans)
    own = tok_rows - window
    ext = tok_rows + window

    def at_head(*block):
        return pl.BlockSpec(block, lambda i, me: (head, 0, 0))

    def full(*block):
        return pl.BlockSpec(block, lambda i, me: (0,) * len(block))

    in_specs = [
        at_head(groups, tok_rows, head_dim),
        pl.BlockSpec((None, 1, window, head_dim), lambda i, me: (0, head, 0, 0)),
        at_head(1, tok_rows, head_dim),
        pl.BlockSpec((None, 1, window, head_dim), lambda i, me: (1, head, 0, 0)),
        at_head(1, tok_rows, head_dim),
        full(q_heads, tok_rows),
        full(1, tok_rows),
    ]
    in_specs += [full(*cotans[0].shape)] * pieces
    in_specs += [full(ext, head_dim)] * len(carry)
    in_specs += [pl.BlockSpec(memory_space=pl.ANY)] * (len(before) + len(passing))
    n_in = 1 + 7 + pieces + len(carry)
    first_block, count = blocks
    unroll = math.gcd(UNROLL, count)
    assert first_block % count == 0
    out_specs = [
        pl.BlockSpec((groups, count * BLOCK, head_dim), lambda i, me: (head, first_block // count, 0))
    ]
    out_shape = [jax.ShapeDtypeStruct(queries.shape, BF16)]
    scratch = [
        pltpu.VMEM((ext, head_dim), BF16),
        pltpu.VMEM((ext, head_dim), BF16),
        pltpu.VMEM((head_dim, ext), BF16),
        pltpu.VMEM((groups, tok_rows, head_dim), BF16),
        pltpu.VMEM((tok_rows // BLOCK, 1, groups * BLOCK), F32),
        pltpu.VMEM((unroll, window + BLOCK, groups * BLOCK), BF16),
    ]
    if closing:
        out_specs += [at_head(1, own, head_dim)] * 2 + [full(window, head_dim)] * 2
        out_specs += [full(2, window, head_dim)]
        out_shape += [jax.ShapeDtypeStruct(keys.shape, BF16)] * 2
        out_shape += [jax.ShapeDtypeStruct((window, head_dim), F32)] * 2
        out_shape += [jax.ShapeDtypeStruct((2, window, head_dim), BF16)]
        scratch += [pltpu.VMEM((ext, head_dim), F32)] * 2
    else:
        out_specs += [full(ext, head_dim)] * 2
        out_shape += [jax.ShapeDtypeStruct((ext, head_dim), F32)] * 2
    aliases = {n_in + i: i for i in range(len(before))}
    for i, array in enumerate(passing):
        aliases[n_in + len(before) + i] = len(out_shape)
        out_shape.append(jax.ShapeDtypeStruct(array.shape, array.dtype))
        out_specs.append(pl.BlockSpec(memory_space=pl.ANY))
    pairs = groups * count * BLOCK * (window + BLOCK)
    return pl.pallas_call(
        functools.partial(
            head_kernel, head, blocks, len(carry) // 2, closing, len(before), len(passing)
        ),
        grid_spec=pltpu.PrefetchScalarGridSpec(
            num_scalar_prefetch=1,
            grid=(1,),
            in_specs=in_specs,
            out_specs=out_specs,
            scratch_shapes=scratch,
        ),
        out_shape=out_shape,
        input_output_aliases=aliases,
        compiler_params=pltpu.CompilerParams(vmem_limit_bytes=VMEM_LIMIT),
        cost_estimate=pl.CostEstimate(
            flops=10 * pairs * head_dim, bytes_accessed=8 * tok_rows * head_dim * 2, transcendentals=pairs
        ),
        name="head_backward",
    )(me, queries, rims, keys, rims, values, lse, start, *cotans, *carry, *before, *passing)


def join_kernel(dk_tail_ref, dv_tail_ref, back_ref, dk_in, dv_in, dk_ref, dv_ref):
    dk_ref[0] = (dk_tail_ref[...] + back_ref[0].astype(F32)).astype(BF16)
    dv_ref[0] = (dv_tail_ref[...] + back_ref[1].astype(F32)).astype(BF16)


def join_call(head, dk_tail, dv_tail, back, grad_keys, grad_values):
    window, head_dim = dk_tail.shape
    last = grad_keys.shape[1] // window - 1
    tail = pl.BlockSpec((window, head_dim), lambda i: (0, 0))
    out = pl.BlockSpec((1, window, head_dim), lambda i: (head, last, 0))
    return pl.pallas_call(
        join_kernel,
        grid=(1,),
        in_specs=[
            tail,
            tail,
            pl.BlockSpec((2, window, head_dim), lambda i: (0, 0, 0)),
            pl.BlockSpec(memory_space=pl.ANY),
            pl.BlockSpec(memory_space=pl.ANY),
        ],
        out_specs=[out, out],
        out_shape=[jax.ShapeDtypeStruct(grad_keys.shape, BF16)] * 2,
        input_output_aliases={3: 0, 4: 1},
        name="join_tail",
    )(dk_tail, dv_tail, back, grad_keys, grad_values)


def body(queries, key_states, value_states, attn_output, out_cotangent, logsumexp, doc_start):
    kv_heads, tok_rows, head_dim = key_states.shape
    groups = queries.shape[0] // kv_heads
    pieces = lax.axis_size("head")
    me = lax.axis_index("head").astype(jnp.int32)[None]
    start = doc_start[None, :] - lax.axis_index("ctx") * tok_rows + W
    steps = tok_rows // BLOCK

    def sent(block, distance):
        route = [(i, (i + distance) % pieces) for i in range(pieces)]
        return lax.ppermute(block, "head", route)

    def packed(head, after):
        return pack_call(
            head, me, out_cotangent, attn_output, kv_heads, groups * head_dim, pieces, after
        )

    def arrived(parts):
        return [part if k == 0 else sent(part, k) for k, part in enumerate(parts)]

    parts = {0: packed(0, out_cotangent)}
    cotans = {0: arrived(parts[0])}
    rims = from_behind(rim_call(key_states, value_states, parts[0][0]), "ctx", 1)
    after = parts[0][0]
    for head in range(kv_heads - 1, 0, -1):
        parts[head] = packed(head, after)
        after = parts[head][0]
    if kv_heads > 1:
        cotans[1] = arrived(parts[1])

    before = []
    waiting = None
    for head in range(kv_heads):
        later = parts[head + 2] if head + 2 < kv_heads else []
        got = head_call(
            head, (0, steps), me, queries, rims, key_states, value_states,
            logsumexp, start, cotans[head], before, [], True, later[1:],
        )
        if later:
            cotans[head + 2] = arrived([later[0], *got[6:]])
        before = list(got[:3])
        if waiting is not None:
            before[1:] = join_call(*waiting, *before[1:])
        waiting = (head, got[3], got[4], from_behind(got[5], "ctx", -1))
    before[1:] = join_call(*waiting, *before[1:])
    return tuple(before)


def solution(mesh):
    return jax.shard_map(
        body,
        mesh=mesh,
        in_specs=(
            P("head", "ctx", None),
            P("head", "ctx", None),
            P("head", "ctx", None),
            P(("ctx", "head"), None),
            P(("ctx", "head"), None),
            P("head", "ctx"),
            P("ctx"),
        ),
        out_specs=(P("head", "ctx", None), P("head", "ctx", None), P("head", "ctx", None)),
        check_vma=False,
    )
```

```python
import functools
import math

import jax
import jax.numpy as jnp
from jax import lax
from jax.experimental import pallas as pl
from jax.experimental.pallas import tpu as pltpu
from jax.sharding import PartitionSpec as P

W = 1024
QPRE = 168
BLOCK = 128
SUB = 32
UNROLL = 4
VMEM_LIMIT = 56 * 1024 * 1024
LOG2E = math.log2(math.e)
F32 = jnp.float32
BF16 = jnp.bfloat16
NT = (((1,), (1,)), ((), ()))
NN = (((1,), (0,)), ((), ()))


def from_behind(block, axis, distance):
    devices = range(lax.axis_size(axis))
    route = [(i - distance, i) for i in devices if i - distance in devices]
    return lax.ppermute(block, axis, route)


def pack_kernel(pieces, ends, me_ref, *refs):
    cotan_refs, output_refs = refs[:pieces], refs[pieces : 2 * pieces]
    end_refs = refs[2 * pieces : 2 * pieces + ends]
    refs = refs[2 * pieces + ends + 1 :]
    out_refs, rows_ref = refs[:pieces], refs[-1]
    for i in range(ends):
        refs[pieces][i] = end_refs[i][...]
    rows, cols = cotan_refs[0].shape
    groups = cols // BLOCK
    in_piece = rows // BLOCK
    head_of = lax.broadcasted_iota(jnp.int32, (16, cols), 1) // BLOCK
    member = (head_of == lax.broadcasted_iota(jnp.int32, (16, cols), 0)).astype(BF16)
    rows_ref[...] = jnp.zeros_like(rows_ref)
    for k in range(pieces):
        cotan = cotan_refs[k][...]
        product = cotan.astype(F32) * output_refs[k][...].astype(F32)
        high = product.astype(BF16)
        low = (product - high.astype(F32)).astype(BF16)
        delta = lax.dot_general(member, high, NT, preferred_element_type=F32)
        delta = delta + lax.dot_general(member, low, NT, preferred_element_type=F32)
        out_refs[k][:rows] = cotan
        for part in range(3):
            rounded = delta.astype(BF16).astype(F32)
            delta = delta - rounded
            for j in range(in_piece):
                for i in range(groups):
                    rows_ref[
                        part * in_piece + j : part * in_piece + j + 1, i * BLOCK : (i + 1) * BLOCK
                    ] = rounded[i : i + 1, j * BLOCK : (j + 1) * BLOCK]
        out_refs[k][rows:] = rows_ref[...].astype(BF16)


def pack_call(head, me, cotan, output, kv_heads, cols, pieces, after, ends=(), ends_of=0):
    rows = cotan.shape[0]
    assert 3 * (rows // BLOCK) <= 16

    def piece_at(k):
        return pl.BlockSpec(
            (rows, cols), lambda i, me: (0, lax.rem(me[0] + k, pieces) * kv_heads + head)
        )

    in_specs = [piece_at(k) for k in range(pieces)] * 2
    for array in ends:
        last = array.shape[1] // W - 1
        in_specs += [pl.BlockSpec((ends_of, W, array.shape[2]), lambda i, me: (0, last, 0))]
    in_specs += [pl.BlockSpec(memory_space=pl.ANY)]
    operands = [cotan] * pieces + [output] * pieces + [*ends, after]
    out_specs = [pl.BlockSpec((rows + 16, cols), lambda i, me: (0, 0))] * pieces
    out_shape = [jax.ShapeDtypeStruct((rows + 16, cols), BF16)] * pieces
    if ends:
        shape = (len(ends), ends_of, W, ends[0].shape[2])
        out_specs += [pl.BlockSpec(shape, lambda i, me: (0, 0, 0, 0))]
        out_shape += [jax.ShapeDtypeStruct(shape, BF16)]
    scratch = [pltpu.VMEM((16, cols), F32)]
    return pl.pallas_call(
        functools.partial(pack_kernel, pieces, len(ends)),
        grid_spec=pltpu.PrefetchScalarGridSpec(
            num_scalar_prefetch=1,
            grid=(1,),
            in_specs=in_specs,
            out_specs=out_specs,
            scratch_shapes=scratch,
        ),
        out_shape=out_shape,
        compiler_params=pltpu.CompilerParams(vmem_limit_bytes=VMEM_LIMIT),
        cost_estimate=pl.CostEstimate(
            flops=4 * rows * cols * pieces, bytes_accessed=6 * rows * cols * pieces, transcendentals=0
        ),
        name="pack_cotangent",
    )(me, *operands)


def rim_kernel(key_ref, value_ref, after_ref, out_ref):
    out_ref[0] = key_ref[...]
    out_ref[1] = value_ref[...]


def rim_call(keys, values, from_head, after):
    kv_heads, tok_rows, head_dim = keys.shape
    last = pl.BlockSpec((1, W, head_dim), lambda i: (i + from_head, tok_rows // W - 1, 0))
    return pl.pallas_call(
        rim_kernel,
        grid=(kv_heads - from_head,),
        in_specs=[last, last, pl.BlockSpec(memory_space=pl.ANY)],
        out_specs=pl.BlockSpec((2, 1, W, head_dim), lambda i: (0, i, 0, 0)),
        out_shape=jax.ShapeDtypeStruct((2, kv_heads - from_head, W, head_dim), BF16),
        name="rims",
    )(keys, values, after)


def head_kernel(head, blocks, carried, aliased, passed, me_ref, *refs):
    q_ref, kh_ref, ko_ref, vh_ref, vo_ref, lse_ref, start_ref = refs[:7]
    groups, _, head_dim = q_ref.shape
    window = kh_ref.shape[0]
    tok_rows = ko_ref.shape[1]
    first_block, count = blocks
    opening = first_block == 0
    closing = first_block + count == tok_rows // BLOCK
    outputs = 1 + (4 if closing else 2) + opening
    pieces = len(refs) - 7 - 2 * carried - aliased - 2 * passed - outputs - 8
    cotan_refs = refs[7 : 7 + pieces]
    refs = refs[7 + pieces :]
    carry_refs = refs[: 2 * carried]
    refs = refs[2 * carried + aliased + passed :]
    dq_ref = refs[0]
    k_all, v_all, kt_all, cotan_all, delta_all, ds_all, dk_all, dv_all = refs[outputs + passed :]
    piece_rows = tok_rows // pieces
    in_piece = piece_rows // BLOCK
    span = window + BLOCK
    cols = groups * BLOCK
    scale = QPRE ** (-0.5)
    me = me_ref[0]
    base = first_block * BLOCK
    extent = k_all.shape[0]
    in_rim = max(window - base, 0)

    for all_ref, rim_ref, own_ref in ((k_all, kh_ref, ko_ref), (v_all, vh_ref, vo_ref)):
        if in_rim:
            all_ref[:in_rim] = rim_ref[base:]
        skip = base + in_rim - window
        all_ref[in_rim:] = own_ref[0, skip : skip + extent - in_rim]
    unit = (
        lax.broadcasted_iota(jnp.int32, (head_dim, head_dim), 0)
        == lax.broadcasted_iota(jnp.int32, (head_dim, head_dim), 1)
    ).astype(BF16)
    kt_all[...] = lax.dot_general(unit, k_all[...], NT, preferred_element_type=F32).astype(BF16)
    dk_all[...] = jnp.zeros_like(dk_all)
    dv_all[...] = jnp.zeros_like(dv_all)
    for all_ref, carry_ref in zip((dk_all, dv_all), carry_refs):
        all_ref[: carry_ref.shape[0]] = carry_ref[...]
    ds_all[...] = jnp.zeros_like(ds_all)
    for i in range(pieces):
        source = lax.rem(me - i + pieces, pieces)
        where = pl.ds(pl.multiple_of(source * piece_rows, piece_rows), piece_rows)
        for j in range(groups):
            cotan_all[j, where, :] = cotan_refs[i][:piece_rows, j * head_dim : (j + 1) * head_dim]
        parts = cotan_refs[i][piece_rows:].astype(F32)
        for j in range(in_piece):
            row = parts[j : j + 1] + parts[in_piece + j : in_piece + j + 1]
            delta_all[source * in_piece + j] = row + parts[2 * in_piece + j : 2 * in_piece + j + 1]

    def write_query(first, slot):
        dq = lax.dot_general(
            kt_all[:, pl.ds(first, span)], ds_all[slot], NN, preferred_element_type=F32
        )
        dq = (dq.T * F32(scale)).astype(BF16)
        dq_ref[:, pl.ds(first, BLOCK), :] = dq.reshape(groups, BLOCK, head_dim)

    token = lax.broadcasted_iota(jnp.int32, (1, cols), 1) % BLOCK
    place = lax.broadcasted_iota(jnp.int32, (SUB, cols), 0)
    chunks = span // BLOCK
    unroll = ds_all.shape[0]

    def load(index):
        first = pl.multiple_of(index * BLOCK, BLOCK)
        token_first = pl.multiple_of(base + first, BLOCK)
        here = pl.ds(token_first, BLOCK)
        query = q_ref[:, pl.ds(first, BLOCK), :].reshape(cols, head_dim)
        cotan = cotan_all[:, here, :].reshape(cols, head_dim)
        rows = [lse_ref[head * groups + i : head * groups + i + 1, here] for i in range(groups)]
        lse = jnp.concatenate(rows, axis=1) * F32(LOG2E)
        delta = delta_all[first_block + index]
        start = jnp.concatenate([start_ref[:, here]] * groups, axis=1) - token_first
        lower = jnp.maximum(start, token + 1)
        return first, query, cotan, lse, delta, lower

    def span_of(first, i):
        return pl.ds(pl.multiple_of(first + i * BLOCK, BLOCK), BLOCK)

    def front(block, i):
        first, query, cotan = block[:3]
        rows = span_of(first, i)
        return (
            lax.dot_general(k_all[rows, :], query, NT, preferred_element_type=F32),
            lax.dot_general(v_all[rows, :], cotan, NT, preferred_element_type=F32),
        )

    def back(block, i, probs_low, dscores):
        first, query, cotan = block[:3]
        rows = span_of(first, i)
        dv_all[rows, :] += lax.dot_general(probs_low, cotan, NN, preferred_element_type=F32)
        dk_all[rows, :] += lax.dot_general(dscores, query, NN, preferred_element_type=F32)

    def middle(block, slot, i, scores, dprobs):
        _, _, _, lse, delta, lower = block
        lows = []
        for at in range(0, BLOCK, SUB):
            part = slice(at, at + SUB)
            shift = i * BLOCK + at
            allowed = place >= lower - shift
            if shift + SUB > window:
                allowed = allowed & (place <= token + (window - shift))
            probs = jnp.where(
                allowed, jnp.exp2(scores[part] * F32(scale * LOG2E) - lse), F32(0.0)
            )
            dscores = (probs * (dprobs[part] - delta)).astype(BF16)
            ds_all[slot, shift : shift + SUB, :] = dscores
            lows.append((probs.astype(BF16), dscores))
        probs_low = jnp.concatenate([x for x, _ in lows], axis=0)
        dscores = jnp.concatenate([x for _, x in lows], axis=0)
        return probs_low, dscores

    def some_blocks(index, nothing):
        blocks = [load(unroll * index + j) for j in range(unroll)]
        stages = [(j, i) for j in range(unroll) for i in range(chunks)]
        ready = front(blocks[0], 0)
        before = jnp.maximum(unroll * index - 1, 0)
        write_query(pl.multiple_of(before * BLOCK, BLOCK), unroll - 1)
        held = None
        for n, (j, i) in enumerate(stages):
            scores, dprobs = ready
            if n + 1 < len(stages):
                jj, ii = stages[n + 1]
                ready = front(blocks[jj], ii)
            if held is not None:
                back(*held)
            if i == 1 and j > 0:
                write_query(blocks[j - 1][0], j - 1)
            held = (blocks[j], i, *middle(blocks[j], j, i, scores, dprobs))
        back(*held)
        return nothing

    lax.fori_loop(0, count // unroll, some_blocks, 0)
    write_query((count - 1) * BLOCK, unroll - 1)

    if closing:
        dk_ref, dv_ref, dk_tail_ref, dv_tail_ref = refs[1:5]
        tail = extent - window
        own = tail - dk_ref.shape[1]
        dk_ref[0] = (dk_all[own:tail] * F32(scale)).astype(BF16)
        dv_ref[0] = dv_all[own:tail].astype(BF16)
        dk_tail_ref[0] = dk_all[tail:] * F32(scale)
        dv_tail_ref[0] = dv_all[tail:]
    else:
        dk_next_ref, dv_next_ref = refs[1:3]
        dk_next_ref[...] = dk_all[extent - window :]
        dv_next_ref[...] = dv_all[extent - window :]
    if opening:
        halo_ref = refs[outputs - 1]
        halo_ref[0, 0] = (dk_all[:window] * F32(scale)).astype(BF16)
        halo_ref[0, 1] = dv_all[:window].astype(BF16)


def head_call(
    head, blocks, me, queries, rims, rim_head, keys, values, lse, start, cotans, before, carry, passing, halos=1
):
    kv_heads, tok_rows, head_dim = keys.shape
    q_heads = queries.shape[0]
    groups = q_heads // kv_heads
    window = rims.shape[2]
    pieces = len(cotans)
    own = tok_rows - window
    first_block, count = blocks
    assert first_block % count == 0
    extent = count * BLOCK + window

    def at_head(*block):
        return pl.BlockSpec(block, lambda i, me: (head, 0, 0))

    def full(*block):
        return pl.BlockSpec(block, lambda i, me: (0,) * len(block))

    q_spec = pl.BlockSpec(
        (groups, count * BLOCK, head_dim), lambda i, me: (head, first_block // count, 0)
    )
    in_specs = [
        q_spec,
        pl.BlockSpec((None, None, window, head_dim), lambda i, me: (0, rim_head, 0, 0)),
        at_head(1, tok_rows, head_dim),
        pl.BlockSpec((None, None, window, head_dim), lambda i, me: (1, rim_head, 0, 0)),
        at_head(1, tok_rows, head_dim),
        full(q_heads, tok_rows),
        full(1, tok_rows),
    ]
    in_specs += [full(*cotans[0].shape)] * pieces
    in_specs += [full(*array.shape) for array in carry]
    in_specs += [pl.BlockSpec(memory_space=pl.ANY)] * (len(before) + len(passing))
    n_in = 1 + 7 + pieces + len(carry)
    unroll = math.gcd(UNROLL, count)
    out_specs = [q_spec]
    out_shape = [jax.ShapeDtypeStruct(queries.shape, BF16)]
    if first_block + count == tok_rows // BLOCK:
        out_specs += [at_head(1, own, head_dim)] * 2 + [at_head(1, window, head_dim)] * 2
        out_shape += [jax.ShapeDtypeStruct(keys.shape, BF16)] * 2
        out_shape += [jax.ShapeDtypeStruct((kv_heads, window, head_dim), F32)] * 2
    else:
        out_specs += [full(window, head_dim)] * 2
        out_shape += [jax.ShapeDtypeStruct((window, head_dim), F32)] * 2
    if first_block == 0:
        at = head if halos > 1 else 0
        out_specs += [pl.BlockSpec((1, 2, window, head_dim), lambda i, me: (at, 0, 0, 0))]
        out_shape += [jax.ShapeDtypeStruct((halos, 2, window, head_dim), BF16)]
    scratch = [
        pltpu.VMEM((extent, head_dim), BF16),
        pltpu.VMEM((extent, head_dim), BF16),
        pltpu.VMEM((head_dim, extent), BF16),
        pltpu.VMEM((groups, tok_rows, head_dim), BF16),
        pltpu.VMEM((tok_rows // BLOCK, 1, groups * BLOCK), F32),
        pltpu.VMEM((unroll, window + BLOCK, groups * BLOCK), BF16),
        pltpu.VMEM((extent, head_dim), F32),
        pltpu.VMEM((extent, head_dim), F32),
    ]
    aliases = {n_in + i: i for i in range(len(before))}
    for i, array in enumerate(passing):
        aliases[n_in + len(before) + i] = len(out_shape)
        out_shape.append(jax.ShapeDtypeStruct(array.shape, array.dtype))
        out_specs.append(pl.BlockSpec(memory_space=pl.ANY))
    pairs = groups * count * BLOCK * (window + BLOCK)
    return pl.pallas_call(
        functools.partial(
            head_kernel, head, blocks, len(carry) // 2, len(before), len(passing)
        ),
        grid_spec=pltpu.PrefetchScalarGridSpec(
            num_scalar_prefetch=1,
            grid=(1,),
            in_specs=in_specs,
            out_specs=out_specs,
            scratch_shapes=scratch,
        ),
        out_shape=out_shape,
        input_output_aliases=aliases,
        compiler_params=pltpu.CompilerParams(vmem_limit_bytes=VMEM_LIMIT),
        cost_estimate=pl.CostEstimate(
            flops=40 * pairs * head_dim, bytes_accessed=8 * tok_rows, transcendentals=0
        ),
        name="head_backward",
    )(me, queries, rims, keys, rims, values, lse, start, *cotans, *carry, *before, *passing)


def join_kernel(joint, dk_tail_ref, dv_tail_ref, *refs):
    backs = refs[:-4]
    dk_ref, dv_ref = refs[-2:]

    def join(back_ref):
        dk_ref[...] = (dk_tail_ref[...] + back_ref[:, 0].astype(F32)).astype(BF16)
        dv_ref[...] = (dv_tail_ref[...] + back_ref[:, 1].astype(F32)).astype(BF16)

    if len(backs) == 1:
        join(backs[0])
    else:
        pl.when(pl.program_id(0) < joint)(lambda: join(backs[0]))
        pl.when(pl.program_id(0) >= joint)(lambda: join(backs[1]))


def join_call(dk_tail, dv_tail, backs, grad_keys, grad_values):
    kv_heads, window, head_dim = dk_tail.shape
    last = grad_keys.shape[1] // window - 1
    joint = backs[0].shape[0]
    tail = pl.BlockSpec((1, window, head_dim), lambda i: (i, 0, 0))
    out = pl.BlockSpec((1, window, head_dim), lambda i: (i, last, 0))
    anywhere = pl.BlockSpec(memory_space=pl.ANY)
    shape = (1, 2, window, head_dim)
    back_specs = [pl.BlockSpec(shape, lambda i: (jnp.minimum(i, joint - 1), 0, 0, 0))]
    back_specs += [pl.BlockSpec(shape, lambda i: (0, 0, 0, 0))] * (len(backs) - 1)
    return pl.pallas_call(
        functools.partial(join_kernel, joint),
        grid=(kv_heads,),
        in_specs=[tail, tail, *back_specs, anywhere, anywhere],
        out_specs=[out, out],
        out_shape=[jax.ShapeDtypeStruct(grad_keys.shape, BF16)] * 2,
        input_output_aliases={2 + len(backs): 0, 3 + len(backs): 1},
        compiler_params=pltpu.CompilerParams(vmem_limit_bytes=VMEM_LIMIT),
        name="join_tails",
    )(dk_tail, dv_tail, *backs, grad_keys, grad_values)


def body(queries, key_states, value_states, attn_output, out_cotangent, logsumexp, doc_start):
    kv_heads, tok_rows, head_dim = key_states.shape
    groups = queries.shape[0] // kv_heads
    pieces = lax.axis_size("head")
    me = lax.axis_index("head").astype(jnp.int32)[None]
    start = doc_start[None, :] - lax.axis_index("ctx") * tok_rows + W
    steps = tok_rows // BLOCK

    def sent(block, distance):
        route = [(i, (i + distance) % pieces) for i in range(pieces)]
        return lax.ppermute(block, "head", route)

    def packed(head, after, *ends):
        return pack_call(
            head, me, out_cotangent, attn_output, kv_heads, groups * head_dim, pieces, after, *ends
        )

    def arrived(parts):
        return [part if k == 0 else sent(part, k) for k, part in enumerate(parts)]

    early = (kv_heads + 1) // 2
    *first, ends = packed(0, out_cotangent, (key_states, value_states), early)
    parts = {0: first}
    cotans = {0: arrived(first)}
    rims = [from_behind(ends, "ctx", 1)]
    after = first[0]
    for head in range(kv_heads - 1, 0, -1):
        parts[head] = packed(head, after)
        after = parts[head][0]
    if kv_heads > 1:
        held = lax.optimization_barrier((*parts[1], *cotans[0][1:]))
        parts[1], cotans[0][1:] = list(held[:pieces]), held[pieces:]
        cotans[1] = arrived(parts[1])
    if kv_heads > early:
        ends = rim_call(key_states, value_states, early, after)
        rims.append(from_behind(ends, "ctx", 1))

    split = 2 * W == tok_rows
    joint = kv_heads - 1 if split else kv_heads
    before = []
    backs = []
    for head in range(kv_heads):
        later = parts[head + 2] if head + 2 < kv_heads else []
        call = functools.partial(
            head_call, head, me=me, queries=queries, rims=rims[head // early], rim_head=head % early,
            keys=key_states, values=value_states, lse=logsumexp, start=start, cotans=cotans[head],
        )
        if head < joint:
            got = call((0, steps), before=before, carry=[], passing=later[1:], halos=joint)
            if later:
                moving = list(got[6:])
                held = lax.optimization_barrier((*[moving[i - 1] for i in (pieces // 2,)], *cotans[head + 1][1:]))
                for i, array in zip((pieces // 2,), held):
                    moving[i - 1] = array
                cotans[head + 1][1:] = held[len((pieces // 2,)) :]
                cotans[head + 2] = arrived([later[0], *moving])
            before = list(got[:6])
            if head == joint - 1:
                backs.append(from_behind(got[5], "ctx", -1))
        else:
            dq, *carry, halo = call((0, steps // 2), before=before[:1], carry=[], passing=[])
            backs.append(from_behind(halo, "ctx", -1))
            before = call((steps // 2, steps // 2), before=[dq, *before[1:5]], carry=carry, passing=[])
    grad_queries, grad_keys, grad_values, *tails = before[:5]
    grad_keys, grad_values = join_call(*tails, backs, grad_keys, grad_values)
    return grad_queries, grad_keys, grad_values


def solution(mesh):
    return jax.shard_map(
        body,
        mesh=mesh,
        in_specs=(
            P("head", "ctx", None),
            P("head", "ctx", None),
            P("head", "ctx", None),
            P(("ctx", "head"), None),
            P(("ctx", "head"), None),
            P("head", "ctx"),
            P("ctx"),
        ),
        out_specs=(P("head", "ctx", None), P("head", "ctx", None), P("head", "ctx", None)),
        check_vma=False,
    )
```

```python
import functools
import math

import jax
import jax.numpy as jnp
from jax import lax
from jax.experimental import pallas as pl
from jax.experimental.pallas import tpu as pltpu
from jax.sharding import PartitionSpec as P

W = 1024
QPRE = 168
BLOCK = 128
SUB = 32
UNROLL = 8
VMEM_LIMIT = 60 * 1024 * 1024
LOG2E = math.log2(math.e)
F32 = jnp.float32
BF16 = jnp.bfloat16
NT = (((1,), (1,)), ((), ()))
NN = (((1,), (0,)), ((), ()))


def from_behind(block, axis, distance):
    devices = range(lax.axis_size(axis))
    route = [(i - distance, i) for i in devices if i - distance in devices]
    return lax.ppermute(block, axis, route)


def pack_kernel(pieces, ends, me_ref, *refs):
    cotan_refs, output_refs = refs[:pieces], refs[pieces : 2 * pieces]
    end_refs = refs[2 * pieces : 2 * pieces + ends]
    refs = refs[2 * pieces + ends + 1 :]
    out_refs, rows_ref = refs[:pieces], refs[-1]
    for i in range(ends):
        refs[pieces][i] = end_refs[i][...]
    rows, cols = cotan_refs[0].shape
    groups = cols // BLOCK
    in_piece = rows // BLOCK
    head_of = lax.broadcasted_iota(jnp.int32, (16, cols), 1) // BLOCK
    member = (head_of == lax.broadcasted_iota(jnp.int32, (16, cols), 0)).astype(BF16)
    rows_ref[...] = jnp.zeros_like(rows_ref)
    for k in range(pieces):
        cotan = cotan_refs[k][...]
        product = cotan.astype(F32) * output_refs[k][...].astype(F32)
        high = product.astype(BF16)
        low = (product - high.astype(F32)).astype(BF16)
        delta = lax.dot_general(member, high, NT, preferred_element_type=F32)
        delta = delta + lax.dot_general(member, low, NT, preferred_element_type=F32)
        out_refs[k][:rows] = cotan
        for part in range(3):
            rounded = delta.astype(BF16).astype(F32)
            delta = delta - rounded
            for j in range(in_piece):
                for i in range(groups):
                    rows_ref[
                        part * in_piece + j : part * in_piece + j + 1, i * BLOCK : (i + 1) * BLOCK
                    ] = rounded[i : i + 1, j * BLOCK : (j + 1) * BLOCK]
        out_refs[k][rows:] = rows_ref[...].astype(BF16)


def pack_call(head, me, cotan, output, kv_heads, cols, pieces, after, ends=(), ends_of=0):
    rows = cotan.shape[0]
    assert 3 * (rows // BLOCK) <= 16

    def piece_at(k):
        return pl.BlockSpec(
            (rows, cols), lambda i, me: (0, lax.rem(me[0] + k, pieces) * kv_heads + head)
        )

    in_specs = [piece_at(k) for k in range(pieces)] * 2
    for array in ends:
        last = array.shape[1] // W - 1
        in_specs += [pl.BlockSpec((ends_of, W, array.shape[2]), lambda i, me: (0, last, 0))]
    in_specs += [pl.BlockSpec(memory_space=pl.ANY)]
    operands = [cotan] * pieces + [output] * pieces + [*ends, after]
    out_specs = [pl.BlockSpec((rows + 16, cols), lambda i, me: (0, 0))] * pieces
    out_shape = [jax.ShapeDtypeStruct((rows + 16, cols), BF16)] * pieces
    if ends:
        shape = (len(ends), ends_of, W, ends[0].shape[2])
        out_specs += [pl.BlockSpec(shape, lambda i, me: (0, 0, 0, 0))]
        out_shape += [jax.ShapeDtypeStruct(shape, BF16)]
    scratch = [pltpu.VMEM((16, cols), F32)]
    return pl.pallas_call(
        functools.partial(pack_kernel, pieces, len(ends)),
        grid_spec=pltpu.PrefetchScalarGridSpec(
            num_scalar_prefetch=1,
            grid=(1,),
            in_specs=in_specs,
            out_specs=out_specs,
            scratch_shapes=scratch,
        ),
        out_shape=out_shape,
        compiler_params=pltpu.CompilerParams(vmem_limit_bytes=VMEM_LIMIT),
        cost_estimate=pl.CostEstimate(
            flops=4 * rows * cols * pieces, bytes_accessed=6 * rows * cols * pieces, transcendentals=0
        ),
        name="pack_cotangent",
    )(me, *operands)


def rim_kernel(key_ref, value_ref, after_ref, out_ref):
    out_ref[0] = key_ref[...]
    out_ref[1] = value_ref[...]


def rim_call(keys, values, from_head, after):
    kv_heads, tok_rows, head_dim = keys.shape
    last = pl.BlockSpec((1, W, head_dim), lambda i: (i + from_head, tok_rows // W - 1, 0))
    return pl.pallas_call(
        rim_kernel,
        grid=(kv_heads - from_head,),
        in_specs=[last, last, pl.BlockSpec(memory_space=pl.ANY)],
        out_specs=pl.BlockSpec((2, 1, W, head_dim), lambda i: (0, i, 0, 0)),
        out_shape=jax.ShapeDtypeStruct((2, kv_heads - from_head, W, head_dim), BF16),
        name="rims",
    )(keys, values, after)


def head_kernel(head, window, tok_rows, blocks, carried, aliased, passed, me_ref, *refs):
    q_ref, kh_ref, ko_ref, vh_ref, vo_ref, lse_ref, start_ref = refs[:7]
    groups, _, head_dim = q_ref.shape
    first_block, count = blocks
    opening = first_block == 0
    closing = first_block + count == tok_rows // BLOCK
    outputs = 1 + (4 if closing else 2) + opening
    pieces = len(refs) - 7 - 2 * carried - aliased - 2 * passed - outputs - 8
    cotan_refs = refs[7 : 7 + pieces]
    refs = refs[7 + pieces :]
    carry_refs = refs[: 2 * carried]
    refs = refs[2 * carried + aliased + passed :]
    dq_ref = refs[0]
    k_all, v_all, kt_all, cotan_all, delta_all, ds_all, dk_all, dv_all = refs[outputs + passed :]
    piece_rows = tok_rows // pieces
    in_piece = piece_rows // BLOCK
    span = window + BLOCK
    cols = groups * BLOCK
    scale = QPRE ** (-0.5)
    me = me_ref[0]
    base = first_block * BLOCK
    extent = k_all.shape[0]
    in_rim = max(window - base, 0)

    for all_ref, rim_ref, own_ref in ((k_all, kh_ref, ko_ref), (v_all, vh_ref, vo_ref)):
        if in_rim:
            all_ref[:in_rim] = rim_ref[base:]
        skip = base + in_rim - window
        all_ref[in_rim:] = own_ref[0, skip : skip + extent - in_rim]
    unit = (
        lax.broadcasted_iota(jnp.int32, (head_dim, head_dim), 0)
        == lax.broadcasted_iota(jnp.int32, (head_dim, head_dim), 1)
    ).astype(BF16)
    kt_all[...] = lax.dot_general(unit, k_all[...], NT, preferred_element_type=F32).astype(BF16)
    dk_all[...] = jnp.zeros_like(dk_all)
    dv_all[...] = jnp.zeros_like(dv_all)
    for all_ref, carry_ref in zip((dk_all, dv_all), carry_refs):
        all_ref[: carry_ref.shape[0]] = carry_ref[...]
    ds_all[ds_all.shape[0] - 1] = jnp.zeros(ds_all.shape[1:], BF16)
    for i in range(pieces):
        source = lax.rem(me - i + pieces, pieces)
        where = pl.ds(pl.multiple_of(source * piece_rows, piece_rows), piece_rows)
        for j in range(groups):
            cotan_all[j, where, :] = cotan_refs[i][:piece_rows, j * head_dim : (j + 1) * head_dim]
        parts = cotan_refs[i][piece_rows:].astype(F32)
        for j in range(in_piece):
            row = parts[j : j + 1] + parts[in_piece + j : in_piece + j + 1]
            delta_all[source * in_piece + j] = row + parts[2 * in_piece + j : 2 * in_piece + j + 1]

    def write_query(first, slot):
        dq = lax.dot_general(
            kt_all[:, pl.ds(first, span)], ds_all[slot], NN, preferred_element_type=F32
        )
        dq = (dq.T * F32(scale)).astype(BF16)
        dq_ref[:, pl.ds(first, BLOCK), :] = dq.reshape(groups, BLOCK, head_dim)

    token = lax.broadcasted_iota(jnp.int32, (1, cols), 1) % BLOCK
    place = lax.broadcasted_iota(jnp.int32, (SUB, cols), 0)
    chunks = span // BLOCK
    unroll = ds_all.shape[0]

    def load(index):
        first = pl.multiple_of(index * BLOCK, BLOCK)
        token_first = pl.multiple_of(base + first, BLOCK)
        here = pl.ds(token_first, BLOCK)
        query = q_ref[:, pl.ds(first, BLOCK), :].reshape(cols, head_dim)
        cotan = cotan_all[:, here, :].reshape(cols, head_dim)
        rows = [lse_ref[head * groups + i : head * groups + i + 1, here] for i in range(groups)]
        lse = jnp.concatenate(rows, axis=1) * F32(LOG2E)
        delta = delta_all[first_block + index]
        start = jnp.concatenate([start_ref[:, here]] * groups, axis=1) - token_first
        lower = jnp.maximum(start, token + 1)
        return first, query, cotan, lse, delta, lower

    def span_of(first, i):
        return pl.ds(pl.multiple_of(first + i * BLOCK, BLOCK), BLOCK)

    def front(block, i):
        first, query, cotan = block[:3]
        rows = span_of(first, i)
        return (
            lax.dot_general(k_all[rows, :], query, NT, preferred_element_type=F32),
            lax.dot_general(v_all[rows, :], cotan, NT, preferred_element_type=F32),
        )

    def back(block, i, probs_low, dscores):
        first, query, cotan = block[:3]
        rows = span_of(first, i)
        dv_all[rows, :] += lax.dot_general(probs_low, cotan, NN, preferred_element_type=F32)
        dk_all[rows, :] += lax.dot_general(dscores, query, NN, preferred_element_type=F32)

    def middle(block, slot, i, scores, dprobs):
        _, _, _, lse, delta, lower = block
        lows = []
        for at in range(0, BLOCK, SUB):
            part = slice(at, at + SUB)
            shift = i * BLOCK + at
            allowed = place >= lower - shift
            if shift + SUB > window:
                allowed = allowed & (place <= token + (window - shift))
            probs = jnp.where(
                allowed, jnp.exp2(scores[part] * F32(scale * LOG2E) - lse), F32(0.0)
            )
            dscores = (probs * (dprobs[part] - delta)).astype(BF16)
            ds_all[slot, shift : shift + SUB, :] = dscores
            lows.append((probs.astype(BF16), dscores))
        probs_low = jnp.concatenate([x for x, _ in lows], axis=0)
        dscores = jnp.concatenate([x for _, x in lows], axis=0)
        return probs_low, dscores

    def some_blocks(index, nothing):
        blocks = [load(unroll * index + j) for j in range(unroll)]
        stages = [(j, i) for j in range(unroll) for i in range(chunks)]
        ready = front(blocks[0], 0)
        before = jnp.maximum(unroll * index - 1, 0)
        write_query(pl.multiple_of(before * BLOCK, BLOCK), unroll - 1)
        held = None
        for n, (j, i) in enumerate(stages):
            scores, dprobs = ready
            if n + 1 < len(stages):
                jj, ii = stages[n + 1]
                ready = front(blocks[jj], ii)
            if held is not None:
                back(*held)
            if i == 1 and j > 0:
                write_query(blocks[j - 1][0], j - 1)
            held = (blocks[j], i, *middle(blocks[j], j, i, scores, dprobs))
        back(*held)
        return nothing

    lax.fori_loop(0, count // unroll, some_blocks, 0)
    write_query((count - 1) * BLOCK, unroll - 1)

    if closing:
        dk_ref, dv_ref, dk_tail_ref, dv_tail_ref = refs[1:5]
        tail = extent - window
        own = tail - dk_ref.shape[1]
        dk_ref[0] = (dk_all[own:tail] * F32(scale)).astype(BF16)
        dv_ref[0] = dv_all[own:tail].astype(BF16)
        dk_tail_ref[0] = (dk_all[tail:] * F32(scale)).astype(BF16)
        dv_tail_ref[0] = dv_all[tail:].astype(BF16)
    else:
        dk_next_ref, dv_next_ref = refs[1:3]
        dk_next_ref[...] = dk_all[extent - window :]
        dv_next_ref[...] = dv_all[extent - window :]
    if opening:
        halo_ref = refs[outputs - 1]
        halo_ref[0, 0] = (dk_all[:window] * F32(scale)).astype(BF16)
        halo_ref[0, 1] = dv_all[:window].astype(BF16)


def head_call(
    head, blocks, me, queries, rims, rim_head, keys, values, lse, start, cotans, before, carry, passing, halo=None
):
    kv_heads, tok_rows, head_dim = keys.shape
    q_heads = queries.shape[0]
    groups = q_heads // kv_heads
    window = rims.shape[2]
    pieces = len(cotans)
    own = tok_rows - window
    first_block, count = blocks
    assert first_block % count == 0
    extent = count * BLOCK + window
    rim_rows = window if first_block == 0 else BLOCK
    own_rows = min(first_block * BLOCK + extent - window, tok_rows)

    def at_head(*block):
        return pl.BlockSpec(block, lambda i, me: (head, 0, 0))

    def full(*block):
        return pl.BlockSpec(block, lambda i, me: (0,) * len(block))

    q_spec = pl.BlockSpec(
        (groups, count * BLOCK, head_dim), lambda i, me: (head, first_block // count, 0)
    )
    in_specs = [
        q_spec,
        pl.BlockSpec((None, None, rim_rows, head_dim), lambda i, me: (0, rim_head, 0, 0)),
        at_head(1, own_rows, head_dim),
        pl.BlockSpec((None, None, rim_rows, head_dim), lambda i, me: (1, rim_head, 0, 0)),
        at_head(1, own_rows, head_dim),
        full(q_heads, tok_rows),
        full(1, tok_rows),
    ]
    in_specs += [full(*cotans[0].shape)] * pieces
    in_specs += [full(*array.shape) for array in carry]
    n_in = 1 + 7 + pieces + len(carry)
    aliases = {n_in + i: i for i in range(len(before))}
    unroll = math.gcd(UNROLL, count)
    out_specs = [q_spec]
    out_shape = [jax.ShapeDtypeStruct(queries.shape, BF16)]
    if first_block + count == tok_rows // BLOCK:
        out_specs += [at_head(1, own, head_dim)] * 2 + [at_head(1, window, head_dim)] * 2
        out_shape += [jax.ShapeDtypeStruct(keys.shape, BF16)] * 2
        out_shape += [jax.ShapeDtypeStruct((kv_heads, window, head_dim), BF16)] * 2
    else:
        out_specs += [full(window, head_dim)] * 2
        out_shape += [jax.ShapeDtypeStruct((window, head_dim), F32)] * 2
    if first_block == 0:
        slot, size, earlier = halo
        out_specs += [pl.BlockSpec((1, 2, window, head_dim), lambda i, me: (slot, 0, 0, 0))]
        out_shape += [jax.ShapeDtypeStruct((size, 2, window, head_dim), BF16)]
        if earlier is not None:
            aliases[n_in + len(before)] = len(out_shape) - 1
            before = [*before, earlier]
    scratch = [
        pltpu.VMEM((extent, head_dim), BF16),
        pltpu.VMEM((extent, head_dim), BF16),
        pltpu.VMEM((head_dim, extent), BF16),
        pltpu.VMEM((groups, tok_rows, head_dim), BF16),
        pltpu.VMEM((tok_rows // BLOCK, 1, groups * BLOCK), F32),
        pltpu.VMEM((unroll, window + BLOCK, groups * BLOCK), BF16),
        pltpu.VMEM((extent, head_dim), F32),
        pltpu.VMEM((extent, head_dim), F32),
    ]
    in_specs += [pl.BlockSpec(memory_space=pl.ANY)] * (len(before) + len(passing))
    for i, array in enumerate(passing):
        aliases[n_in + len(before) + i] = len(out_shape)
        out_shape.append(jax.ShapeDtypeStruct(array.shape, array.dtype))
        out_specs.append(pl.BlockSpec(memory_space=pl.ANY))
    pairs = groups * count * BLOCK * (window + BLOCK)
    return pl.pallas_call(
        functools.partial(
            head_kernel, head, window, tok_rows, blocks, len(carry) // 2, len(before), len(passing)
        ),
        grid_spec=pltpu.PrefetchScalarGridSpec(
            num_scalar_prefetch=1,
            grid=(1,),
            in_specs=in_specs,
            out_specs=out_specs,
            scratch_shapes=scratch,
        ),
        out_shape=out_shape,
        input_output_aliases=aliases,
        compiler_params=pltpu.CompilerParams(vmem_limit_bytes=VMEM_LIMIT),
        cost_estimate=pl.CostEstimate(
            flops=40 * pairs * head_dim, bytes_accessed=8 * tok_rows, transcendentals=0
        ),
        name="head_backward",
    )(me, queries, rims, keys, rims, values, lse, start, *cotans, *carry, *before, *passing)


def join_kernel(joint, dk_tail_ref, dv_tail_ref, *refs):
    backs = refs[:-4]
    dk_ref, dv_ref = refs[-2:]

    def join(back_ref):
        dk_ref[...] = (dk_tail_ref[...].astype(F32) + back_ref[:, 0].astype(F32)).astype(BF16)
        dv_ref[...] = (dv_tail_ref[...].astype(F32) + back_ref[:, 1].astype(F32)).astype(BF16)

    if len(backs) == 1:
        join(backs[0])
    else:
        pl.when(pl.program_id(0) < joint)(lambda: join(backs[0]))
        pl.when(pl.program_id(0) >= joint)(lambda: join(backs[1]))


def join_call(dk_tail, dv_tail, backs, grad_keys, grad_values):
    kv_heads, window, head_dim = dk_tail.shape
    last = grad_keys.shape[1] // window - 1
    joint = backs[0].shape[0]
    tail = pl.BlockSpec((1, window, head_dim), lambda i: (i, 0, 0))
    out = pl.BlockSpec((1, window, head_dim), lambda i: (i, last, 0))
    anywhere = pl.BlockSpec(memory_space=pl.ANY)
    shape = (1, 2, window, head_dim)
    back_specs = [pl.BlockSpec(shape, lambda i: (jnp.minimum(i, joint - 1), 0, 0, 0))]
    back_specs += [pl.BlockSpec(shape, lambda i: (0, 0, 0, 0))] * (len(backs) - 1)
    return pl.pallas_call(
        functools.partial(join_kernel, joint),
        grid=(kv_heads,),
        in_specs=[tail, tail, *back_specs, anywhere, anywhere],
        out_specs=[out, out],
        out_shape=[jax.ShapeDtypeStruct(grad_keys.shape, BF16)] * 2,
        input_output_aliases={2 + len(backs): 0, 3 + len(backs): 1},
        compiler_params=pltpu.CompilerParams(vmem_limit_bytes=VMEM_LIMIT),
        name="join_tails",
    )(dk_tail, dv_tail, *backs, grad_keys, grad_values)


def body(queries, key_states, value_states, attn_output, out_cotangent, logsumexp, doc_start):
    kv_heads, tok_rows, head_dim = key_states.shape
    groups = queries.shape[0] // kv_heads
    pieces = lax.axis_size("head")
    me = lax.axis_index("head").astype(jnp.int32)[None]
    start = doc_start[None, :] - lax.axis_index("ctx") * tok_rows + W
    steps = tok_rows // BLOCK

    def sent(block, distance):
        route = [(i, (i + distance) % pieces) for i in range(pieces)]
        return lax.ppermute(block, "head", route)

    def packed(head, after, *ends):
        return pack_call(
            head, me, out_cotangent, attn_output, kv_heads, groups * head_dim, pieces, after, *ends
        )

    def arrived(parts):
        return [part if k == 0 else sent(part, k) for k, part in enumerate(parts)]

    early = (kv_heads + 1) // 2
    *first, ends = packed(0, out_cotangent, (key_states, value_states), early)
    parts = {0: first}
    cotans = {0: arrived(first)}
    rims = [from_behind(ends, "ctx", 1)]
    after = first[0]
    for head in range(kv_heads - 1, 0, -1):
        parts[head] = packed(head, after)
        after = parts[head][0]
    if kv_heads > 1:
        held = lax.optimization_barrier((*parts[1], *cotans[0][1:]))
        parts[1], cotans[0][1:] = list(held[:pieces]), held[pieces:]
        cotans[1] = arrived(parts[1])
    if kv_heads > early:
        ends = rim_call(key_states, value_states, early, after)
        rims.append(from_behind(ends, "ctx", 1))

    split = 2 * W == tok_rows
    final = kv_heads - 1 if split else kv_heads
    before = []
    halos = None
    backs = []
    for head in range(kv_heads):
        later = parts[head + 2] if head + 2 < kv_heads else []
        halo = (head, final, halos) if head < final else (0, 1, None)
        call = functools.partial(
            head_call, head, me=me, queries=queries, rims=rims[int(head >= early)],
            rim_head=head - early * (head >= early), keys=key_states, values=value_states,
            lse=logsumexp, start=start, cotans=cotans[head], halo=halo,
        )
        if head + 1 < kv_heads or not split:
            got = call((0, steps), before=before, carry=[], passing=later[1:])
            if later:
                middle = pieces // 2
                moving = list(got[6:])
                held = lax.optimization_barrier((moving[middle - 1], *cotans[head + 1][1:]))
                moving[middle - 1] = held[0]
                cotans[head + 1][1:] = held[1:]
                cotans[head + 2] = arrived([later[0], *moving])
            before, halos = list(got[:5]), got[5]
        else:
            got = call((0, steps // 2), before=before[:1], carry=[], passing=[])
            halos = got[3]
        if head >= final - 1:
            backs.append(from_behind(halos, "ctx", -1))
        if head + 1 == kv_heads and split:
            before = call(
                (steps // 2, steps // 2), before=[got[0], *before[1:]], carry=got[1:3], passing=[]
            )
    grad_queries, grad_keys, grad_values, *tails = before
    grad_keys, grad_values = join_call(*tails, backs, grad_keys, grad_values)
    return grad_queries, grad_keys, grad_values


def solution(mesh):
    return jax.shard_map(
        body,
        mesh=mesh,
        in_specs=(
            P("head", "ctx", None),
            P("head", "ctx", None),
            P("head", "ctx", None),
            P(("ctx", "head"), None),
            P(("ctx", "head"), None),
            P("head", "ctx"),
            P("ctx"),
        ),
        out_specs=(P("head", "ctx", None), P("head", "ctx", None), P("head", "ctx", None)),
        check_vma=False,
    )
```

```python
import functools
import math

import jax
import jax.numpy as jnp
from jax import lax
from jax.experimental import pallas as pl
from jax.experimental.pallas import tpu as pltpu
from jax.sharding import PartitionSpec as P

W = 1024
QPRE = 168
BLOCK = 128
SUB = 32
UNROLL = 4
VMEM_LIMIT = 60 * 1024 * 1024
LOG2E = math.log2(math.e)
F32 = jnp.float32
BF16 = jnp.bfloat16
NT = (((1,), (1,)), ((), ()))
NN = (((1,), (0,)), ((), ()))


def from_behind(block, axis, distance):
    devices = range(lax.axis_size(axis))
    route = [(i - distance, i) for i in devices if i - distance in devices]
    return lax.ppermute(block, axis, route)


def pack_kernel(pieces, ends, me_ref, *refs):
    cotan_refs, output_refs = refs[:pieces], refs[pieces : 2 * pieces]
    end_refs = refs[2 * pieces : 2 * pieces + ends]
    refs = refs[2 * pieces + ends + 1 :]
    out_refs, rows_ref = refs[:pieces], refs[-1]
    for i in range(ends):
        refs[pieces][i] = end_refs[i][...]
    rows, cols = cotan_refs[0].shape
    groups = cols // BLOCK
    in_piece = rows // BLOCK
    head_of = lax.broadcasted_iota(jnp.int32, (16, cols), 1) // BLOCK
    member = (head_of == lax.broadcasted_iota(jnp.int32, (16, cols), 0)).astype(BF16)
    rows_ref[...] = jnp.zeros_like(rows_ref)
    for k in range(pieces):
        cotan = cotan_refs[k][...]
        product = cotan.astype(F32) * output_refs[k][...].astype(F32)
        high = product.astype(BF16)
        low = (product - high.astype(F32)).astype(BF16)
        delta = lax.dot_general(member, high, NT, preferred_element_type=F32)
        delta = delta + lax.dot_general(member, low, NT, preferred_element_type=F32)
        out_refs[k][:rows] = cotan
        for part in range(3):
            rounded = delta.astype(BF16).astype(F32)
            delta = delta - rounded
            for j in range(in_piece):
                for i in range(groups):
                    rows_ref[
                        part * in_piece + j : part * in_piece + j + 1, i * BLOCK : (i + 1) * BLOCK
                    ] = rounded[i : i + 1, j * BLOCK : (j + 1) * BLOCK]
        out_refs[k][rows:] = rows_ref[...].astype(BF16)


def pack_call(head, me, cotan, output, kv_heads, cols, pieces, after, ends=(), ends_of=0):
    rows = cotan.shape[0]
    assert 3 * (rows // BLOCK) <= 16

    def piece_at(k):
        return pl.BlockSpec(
            (rows, cols), lambda i, me: (0, lax.rem(me[0] + k, pieces) * kv_heads + head)
        )

    in_specs = [piece_at(k) for k in range(pieces)] * 2
    for array in ends:
        last = array.shape[1] // W - 1
        in_specs += [pl.BlockSpec((ends_of, W, array.shape[2]), lambda i, me: (0, last, 0))]
    in_specs += [pl.BlockSpec(memory_space=pl.ANY)]
    operands = [cotan] * pieces + [output] * pieces + [*ends, after]
    out_specs = [pl.BlockSpec((rows + 16, cols), lambda i, me: (0, 0))] * pieces
    out_shape = [jax.ShapeDtypeStruct((rows + 16, cols), BF16)] * pieces
    if ends:
        shape = (len(ends), ends_of, W, ends[0].shape[2])
        out_specs += [pl.BlockSpec(shape, lambda i, me: (0, 0, 0, 0))]
        out_shape += [jax.ShapeDtypeStruct(shape, BF16)]
    scratch = [pltpu.VMEM((16, cols), F32)]
    return pl.pallas_call(
        functools.partial(pack_kernel, pieces, len(ends)),
        grid_spec=pltpu.PrefetchScalarGridSpec(
            num_scalar_prefetch=1,
            grid=(1,),
            in_specs=in_specs,
            out_specs=out_specs,
            scratch_shapes=scratch,
        ),
        out_shape=out_shape,
        compiler_params=pltpu.CompilerParams(vmem_limit_bytes=VMEM_LIMIT),
        cost_estimate=pl.CostEstimate(
            flops=4 * rows * cols * pieces, bytes_accessed=6 * rows * cols * pieces, transcendentals=0
        ),
        name="pack_cotangent",
    )(me, *operands)


def rim_kernel(key_ref, value_ref, after_ref, out_ref):
    out_ref[0] = key_ref[...]
    out_ref[1] = value_ref[...]


def rim_call(keys, values, from_head, after):
    kv_heads, tok_rows, head_dim = keys.shape
    last = pl.BlockSpec((1, W, head_dim), lambda i: (i + from_head, tok_rows // W - 1, 0))
    return pl.pallas_call(
        rim_kernel,
        grid=(kv_heads - from_head,),
        in_specs=[last, last, pl.BlockSpec(memory_space=pl.ANY)],
        out_specs=pl.BlockSpec((2, 1, W, head_dim), lambda i: (0, i, 0, 0)),
        out_shape=jax.ShapeDtypeStruct((2, kv_heads - from_head, W, head_dim), BF16),
        name="rims",
    )(keys, values, after)


def head_kernel(head, window, tok_rows, blocks, carried, aliased, passed, me_ref, *refs):
    q_ref, kh_ref, ko_ref, vh_ref, vo_ref, lse_ref, start_ref = refs[:7]
    groups, _, head_dim = q_ref.shape
    first_block, count = blocks
    opening = first_block == 0
    closing = first_block + count == tok_rows // BLOCK
    outputs = 1 + (4 if closing else 2) + opening
    pieces = len(refs) - 7 - 2 * carried - aliased - 2 * passed - outputs - 8
    cotan_refs = refs[7 : 7 + pieces]
    refs = refs[7 + pieces :]
    carry_refs = refs[: 2 * carried]
    refs = refs[2 * carried + aliased + passed :]
    dq_ref = refs[0]
    k_all, v_all, kt_all, cotan_all, delta_all, ds_all, dk_all, dv_all = refs[outputs + passed :]
    piece_rows = tok_rows // pieces
    in_piece = piece_rows // BLOCK
    span = window + BLOCK
    cols = groups * BLOCK
    scale = QPRE ** (-0.5)
    me = me_ref[0]
    base = first_block * BLOCK
    extent = k_all.shape[0]
    in_rim = max(window - base, 0)

    for all_ref, rim_ref, own_ref in ((k_all, kh_ref, ko_ref), (v_all, vh_ref, vo_ref)):
        if in_rim:
            all_ref[:in_rim] = rim_ref[base:]
        skip = base + in_rim - window
        all_ref[in_rim:] = own_ref[0, skip : skip + extent - in_rim]
    unit = (
        lax.broadcasted_iota(jnp.int32, (head_dim, head_dim), 0)
        == lax.broadcasted_iota(jnp.int32, (head_dim, head_dim), 1)
    ).astype(BF16)
    kt_all[...] = lax.dot_general(unit, k_all[...], NT, preferred_element_type=F32).astype(BF16)
    dk_all[...] = jnp.zeros_like(dk_all)
    dv_all[...] = jnp.zeros_like(dv_all)
    for all_ref, carry_ref in zip((dk_all, dv_all), carry_refs):
        all_ref[: carry_ref.shape[0]] = carry_ref[...]
    ds_all[ds_all.shape[0] - 1] = jnp.zeros(ds_all.shape[1:], BF16)
    for i in range(pieces):
        source = lax.rem(me - i + pieces, pieces)
        where = pl.ds(pl.multiple_of(source * piece_rows, piece_rows), piece_rows)
        for j in range(groups):
            cotan_all[j, where, :] = cotan_refs[i][:piece_rows, j * head_dim : (j + 1) * head_dim]
        parts = cotan_refs[i][piece_rows:].astype(F32)
        for j in range(in_piece):
            row = parts[j : j + 1] + parts[in_piece + j : in_piece + j + 1]
            delta_all[source * in_piece + j] = row + parts[2 * in_piece + j : 2 * in_piece + j + 1]

    def write_query(first, slot):
        dq = lax.dot_general(
            kt_all[:, pl.ds(first, span)], ds_all[slot], NN, preferred_element_type=F32
        )
        dq = (dq.T * F32(scale)).astype(BF16)
        dq_ref[:, pl.ds(first, BLOCK), :] = dq.reshape(groups, BLOCK, head_dim)

    token = lax.broadcasted_iota(jnp.int32, (1, cols), 1) % BLOCK
    place = lax.broadcasted_iota(jnp.int32, (SUB, cols), 0)
    chunks = span // BLOCK
    unroll = ds_all.shape[0]

    def load(index):
        first = pl.multiple_of(index * BLOCK, BLOCK)
        token_first = pl.multiple_of(base + first, BLOCK)
        here = pl.ds(token_first, BLOCK)
        query = q_ref[:, pl.ds(first, BLOCK), :].reshape(cols, head_dim)
        cotan = cotan_all[:, here, :].reshape(cols, head_dim)
        rows = [lse_ref[head * groups + i : head * groups + i + 1, here] for i in range(groups)]
        lse = jnp.concatenate(rows, axis=1) * F32(LOG2E)
        delta = delta_all[first_block + index]
        start = jnp.concatenate([start_ref[:, here]] * groups, axis=1) - token_first
        lower = jnp.maximum(start, token + 1)
        return first, query, cotan, lse, delta, lower

    def span_of(first, i):
        return pl.ds(pl.multiple_of(first + i * BLOCK, BLOCK), BLOCK)

    def front(block, i):
        first, query, cotan = block[:3]
        rows = span_of(first, i)
        return (
            lax.dot_general(k_all[rows, :], query, NT, preferred_element_type=F32),
            lax.dot_general(v_all[rows, :], cotan, NT, preferred_element_type=F32),
        )

    def back(block, i, probs_low, dscores):
        first, query, cotan = block[:3]
        rows = span_of(first, i)
        dv_all[rows, :] += lax.dot_general(probs_low, cotan, NN, preferred_element_type=F32)
        dk_all[rows, :] += lax.dot_general(dscores, query, NN, preferred_element_type=F32)

    def middle(block, slot, i, scores, dprobs):
        _, _, _, lse, delta, lower = block
        lows = []
        for at in range(0, BLOCK, SUB):
            part = slice(at, at + SUB)
            shift = i * BLOCK + at
            allowed = place >= lower - shift
            if shift + SUB > window:
                allowed = allowed & (place <= token + (window - shift))
            probs = jnp.where(
                allowed, jnp.exp2(scores[part] * F32(scale * LOG2E) - lse), F32(0.0)
            )
            dscores = (probs * (dprobs[part] - delta)).astype(BF16)
            ds_all[slot, shift : shift + SUB, :] = dscores
            lows.append((probs.astype(BF16), dscores))
        probs_low = jnp.concatenate([x for x, _ in lows], axis=0)
        dscores = jnp.concatenate([x for _, x in lows], axis=0)
        return probs_low, dscores

    def some_blocks(index, nothing):
        blocks = [load(unroll * index + j) for j in range(unroll)]
        stages = [(j, i) for j in range(unroll) for i in range(chunks)]
        ready = front(blocks[0], 0)
        before = jnp.maximum(unroll * index - 1, 0)
        write_query(pl.multiple_of(before * BLOCK, BLOCK), unroll - 1)
        held = None
        for n, (j, i) in enumerate(stages):
            scores, dprobs = ready
            if n + 1 < len(stages):
                jj, ii = stages[n + 1]
                ready = front(blocks[jj], ii)
            if held is not None:
                back(*held)
            if i == 1 and j > 0:
                write_query(blocks[j - 1][0], j - 1)
            held = (blocks[j], i, *middle(blocks[j], j, i, scores, dprobs))
        back(*held)
        return nothing

    lax.fori_loop(0, count // unroll, some_blocks, 0)
    write_query((count - 1) * BLOCK, unroll - 1)

    if closing:
        dk_ref, dv_ref, dk_tail_ref, dv_tail_ref = refs[1:5]
        tail = extent - window
        own = tail - dk_ref.shape[1]
        dk_ref[0] = (dk_all[own:tail] * F32(scale)).astype(BF16)
        dv_ref[0] = dv_all[own:tail].astype(BF16)
        dk_tail_ref[0] = (dk_all[tail:] * F32(scale)).astype(BF16)
        dv_tail_ref[0] = dv_all[tail:].astype(BF16)
    else:
        dk_next_ref, dv_next_ref = refs[1:3]
        dk_next_ref[...] = dk_all[extent - window :]
        dv_next_ref[...] = dv_all[extent - window :]
    if opening:
        halo_ref = refs[outputs - 1]
        halo_ref[0, 0] = (dk_all[:window] * F32(scale)).astype(BF16)
        halo_ref[0, 1] = dv_all[:window].astype(BF16)


def head_call(
    head, blocks, me, queries, rims, rim_head, keys, values, lse, start, cotans, before, carry, passing, halo=None
):
    kv_heads, tok_rows, head_dim = keys.shape
    q_heads = queries.shape[0]
    groups = q_heads // kv_heads
    window = rims.shape[2]
    pieces = len(cotans)
    own = tok_rows - window
    first_block, count = blocks
    assert first_block % count == 0
    extent = count * BLOCK + window
    rim_rows = window if first_block == 0 else BLOCK
    own_rows = min(first_block * BLOCK + extent - window, tok_rows)

    def at_head(*block):
        return pl.BlockSpec(block, lambda i, me: (head, 0, 0))

    def full(*block):
        return pl.BlockSpec(block, lambda i, me: (0,) * len(block))

    q_spec = pl.BlockSpec(
        (groups, count * BLOCK, head_dim), lambda i, me: (head, first_block // count, 0)
    )
    in_specs = [
        q_spec,
        pl.BlockSpec((None, None, rim_rows, head_dim), lambda i, me: (0, rim_head, 0, 0)),
        at_head(1, own_rows, head_dim),
        pl.BlockSpec((None, None, rim_rows, head_dim), lambda i, me: (1, rim_head, 0, 0)),
        at_head(1, own_rows, head_dim),
        full(q_heads, tok_rows),
        full(1, tok_rows),
    ]
    in_specs += [full(*cotans[0].shape)] * pieces
    in_specs += [full(*array.shape) for array in carry]
    n_in = 1 + 7 + pieces + len(carry)
    aliases = {n_in + i: i for i in range(len(before))}
    unroll = math.gcd(UNROLL, count)
    out_specs = [q_spec]
    out_shape = [jax.ShapeDtypeStruct(queries.shape, BF16)]
    if first_block + count == tok_rows // BLOCK:
        out_specs += [at_head(1, own, head_dim)] * 2 + [at_head(1, window, head_dim)] * 2
        out_shape += [jax.ShapeDtypeStruct(keys.shape, BF16)] * 2
        out_shape += [jax.ShapeDtypeStruct((kv_heads, window, head_dim), BF16)] * 2
    else:
        out_specs += [full(window, head_dim)] * 2
        out_shape += [jax.ShapeDtypeStruct((window, head_dim), F32)] * 2
    if first_block == 0:
        slot, size, earlier = halo
        out_specs += [pl.BlockSpec((1, 2, window, head_dim), lambda i, me: (slot, 0, 0, 0))]
        out_shape += [jax.ShapeDtypeStruct((size, 2, window, head_dim), BF16)]
        if earlier is not None:
            aliases[n_in + len(before)] = len(out_shape) - 1
            before = [*before, earlier]
    scratch = [
        pltpu.VMEM((extent, head_dim), BF16),
        pltpu.VMEM((extent, head_dim), BF16),
        pltpu.VMEM((head_dim, extent), BF16),
        pltpu.VMEM((groups, tok_rows, head_dim), BF16),
        pltpu.VMEM((tok_rows // BLOCK, 1, groups * BLOCK), F32),
        pltpu.VMEM((unroll, window + BLOCK, groups * BLOCK), BF16),
        pltpu.VMEM((extent, head_dim), F32),
        pltpu.VMEM((extent, head_dim), F32),
    ]
    in_specs += [pl.BlockSpec(memory_space=pl.ANY)] * (len(before) + len(passing))
    for i, array in enumerate(passing):
        aliases[n_in + len(before) + i] = len(out_shape)
        out_shape.append(jax.ShapeDtypeStruct(array.shape, array.dtype))
        out_specs.append(pl.BlockSpec(memory_space=pl.ANY))
    pairs = groups * count * BLOCK * (window + BLOCK)
    return pl.pallas_call(
        functools.partial(
            head_kernel, head, window, tok_rows, blocks, len(carry) // 2, len(before), len(passing)
        ),
        grid_spec=pltpu.PrefetchScalarGridSpec(
            num_scalar_prefetch=1,
            grid=(1,),
            in_specs=in_specs,
            out_specs=out_specs,
            scratch_shapes=scratch,
        ),
        out_shape=out_shape,
        input_output_aliases=aliases,
        compiler_params=pltpu.CompilerParams(vmem_limit_bytes=VMEM_LIMIT),
        cost_estimate=pl.CostEstimate(
            flops=40 * pairs * head_dim, bytes_accessed=8 * tok_rows, transcendentals=0
        ),
        name="head_backward",
    )(me, queries, rims, keys, rims, values, lse, start, *cotans, *carry, *before, *passing)


def join_kernel(joint, dk_tail_ref, dv_tail_ref, *refs):
    backs = refs[:-4]
    dk_ref, dv_ref = refs[-2:]

    def join(back_ref):
        dk_ref[...] = (dk_tail_ref[...].astype(F32) + back_ref[:, 0].astype(F32)).astype(BF16)
        dv_ref[...] = (dv_tail_ref[...].astype(F32) + back_ref[:, 1].astype(F32)).astype(BF16)

    if len(backs) == 1:
        join(backs[0])
    else:
        pl.when(pl.program_id(0) < joint)(lambda: join(backs[0]))
        pl.when(pl.program_id(0) >= joint)(lambda: join(backs[1]))


def join_call(dk_tail, dv_tail, backs, grad_keys, grad_values):
    kv_heads, window, head_dim = dk_tail.shape
    last = grad_keys.shape[1] // window - 1
    joint = backs[0].shape[0]
    tail = pl.BlockSpec((1, window, head_dim), lambda i: (i, 0, 0))
    out = pl.BlockSpec((1, window, head_dim), lambda i: (i, last, 0))
    anywhere = pl.BlockSpec(memory_space=pl.ANY)
    shape = (1, 2, window, head_dim)
    back_specs = [pl.BlockSpec(shape, lambda i: (jnp.minimum(i, joint - 1), 0, 0, 0))]
    back_specs += [pl.BlockSpec(shape, lambda i: (0, 0, 0, 0))] * (len(backs) - 1)
    return pl.pallas_call(
        functools.partial(join_kernel, joint),
        grid=(kv_heads,),
        in_specs=[tail, tail, *back_specs, anywhere, anywhere],
        out_specs=[out, out],
        out_shape=[jax.ShapeDtypeStruct(grad_keys.shape, BF16)] * 2,
        input_output_aliases={2 + len(backs): 0, 3 + len(backs): 1},
        compiler_params=pltpu.CompilerParams(vmem_limit_bytes=VMEM_LIMIT),
        name="join_tails",
    )(dk_tail, dv_tail, *backs, grad_keys, grad_values)


def body(queries, key_states, value_states, attn_output, out_cotangent, logsumexp, doc_start):
    kv_heads, tok_rows, head_dim = key_states.shape
    groups = queries.shape[0] // kv_heads
    pieces = lax.axis_size("head")
    me = lax.axis_index("head").astype(jnp.int32)[None]
    start = doc_start[None, :] - lax.axis_index("ctx") * tok_rows + W
    steps = tok_rows // BLOCK

    def sent(block, distance):
        route = [(i, (i + distance) % pieces) for i in range(pieces)]
        return lax.ppermute(block, "head", route)

    def packed(head, after, *ends):
        return pack_call(
            head, me, out_cotangent, attn_output, kv_heads, groups * head_dim, pieces, after, *ends
        )

    def arrived(parts):
        return [part if k == 0 else sent(part, k) for k, part in enumerate(parts)]

    early = (kv_heads + 1) // 2
    *first, ends = packed(0, out_cotangent, (key_states, value_states), early)
    parts = {0: first}
    cotans = {0: arrived(first)}
    rims = [from_behind(ends, "ctx", 1)]
    after = first[0]
    for head in range(kv_heads - 1, 0, -1):
        parts[head] = packed(head, after)
        after = parts[head][0]
    if kv_heads > 1:
        held = lax.optimization_barrier((*parts[1], *cotans[0][1:]))
        parts[1], cotans[0][1:] = list(held[:pieces]), held[pieces:]
        cotans[1] = arrived(parts[1])
    if kv_heads > early:
        ends = rim_call(key_states, value_states, early, after)
        rims.append(from_behind(ends, "ctx", 1))

    split = 2 * W == tok_rows
    final = kv_heads - 1 if split else kv_heads
    before = []
    halos = None
    backs = []
    for head in range(kv_heads):
        later = parts[head + 2] if head + 2 < kv_heads else []
        halo = (head, final, halos) if head < final else (0, 1, None)
        call = functools.partial(
            head_call, head, me=me, queries=queries, rims=rims[int(head >= early)],
            rim_head=head - early * (head >= early), keys=key_states, values=value_states,
            lse=logsumexp, start=start, cotans=cotans[head], halo=halo,
        )
        if head + 1 < kv_heads or not split:
            got = call((0, steps), before=before, carry=[], passing=later[1:])
            if later:
                middle = pieces // 2
                moving = list(got[6:])
                held = lax.optimization_barrier((moving[middle - 1], *cotans[head + 1][1:]))
                moving[middle - 1] = held[0]
                cotans[head + 1][1:] = held[1:]
                cotans[head + 2] = arrived([later[0], *moving])
            before, halos = list(got[:5]), got[5]
        else:
            got = call((0, steps // 2), before=before[:1], carry=[], passing=[])
            halos = got[3]
        if head >= final - 1:
            backs.append(from_behind(halos, "ctx", -1))
        if head + 1 == kv_heads and split:
            before = call(
                (steps // 2, steps // 2), before=[got[0], *before[1:]], carry=got[1:3], passing=[]
            )
    grad_queries, grad_keys, grad_values, *tails = before
    grad_keys, grad_values = join_call(*tails, backs, grad_keys, grad_values)
    return grad_queries, grad_keys, grad_values


def solution(mesh):
    return jax.shard_map(
        body,
        mesh=mesh,
        in_specs=(
            P("head", "ctx", None),
            P("head", "ctx", None),
            P("head", "ctx", None),
            P(("ctx", "head"), None),
            P(("ctx", "head"), None),
            P("head", "ctx"),
            P("ctx"),
        ),
        out_specs=(P("head", "ctx", None), P("head", "ctx", None), P("head", "ctx", None)),
        check_vma=False,
    )
```

```python
import functools
import math

import jax
import jax.numpy as jnp
from jax import lax
from jax.experimental import pallas as pl
from jax.experimental.pallas import tpu as pltpu
from jax.sharding import PartitionSpec as P

W = 1024
QPRE = 168
BLOCK = 128
SUB = 32
UNROLL = 4
VMEM_LIMIT = 64 * 1024 * 1024 - 131072
LOG2E = math.log2(math.e)
F32 = jnp.float32
BF16 = jnp.bfloat16
NT = (((1,), (1,)), ((), ()))
NN = (((1,), (0,)), ((), ()))


def from_behind(block, axis, distance):
    devices = range(lax.axis_size(axis))
    route = [(i - distance, i) for i in devices if i - distance in devices]
    return lax.ppermute(block, axis, route)


def pack_kernel(pieces, ends, me_ref, *refs):
    cotan_refs, output_refs = refs[:pieces], refs[pieces : 2 * pieces]
    end_refs = refs[2 * pieces : 2 * pieces + ends]
    refs = refs[2 * pieces + ends + 1 :]
    out_refs, rows_ref = refs[:pieces], refs[-1]
    for i in range(ends):
        refs[pieces][i] = end_refs[i][...]
    rows, cols = cotan_refs[0].shape
    groups = cols // BLOCK
    in_piece = rows // BLOCK
    head_of = lax.broadcasted_iota(jnp.int32, (16, cols), 1) // BLOCK
    member = (head_of == lax.broadcasted_iota(jnp.int32, (16, cols), 0)).astype(BF16)
    rows_ref[...] = jnp.zeros_like(rows_ref)
    for k in range(pieces):
        cotan = cotan_refs[k][...]
        product = cotan.astype(F32) * output_refs[k][...].astype(F32)
        high = product.astype(BF16)
        low = (product - high.astype(F32)).astype(BF16)
        delta = lax.dot_general(member, high, NT, preferred_element_type=F32)
        delta = delta + lax.dot_general(member, low, NT, preferred_element_type=F32)
        out_refs[k][:rows] = cotan
        for part in range(3):
            rounded = delta.astype(BF16).astype(F32)
            delta = delta - rounded
            for j in range(in_piece):
                for i in range(groups):
                    rows_ref[
                        part * in_piece + j : part * in_piece + j + 1, i * BLOCK : (i + 1) * BLOCK
                    ] = rounded[i : i + 1, j * BLOCK : (j + 1) * BLOCK]
        out_refs[k][rows:] = rows_ref[...].astype(BF16)


def pack_call(head, me, cotan, output, kv_heads, cols, pieces, after, ends=(), ends_of=0):
    rows = cotan.shape[0]
    assert 3 * (rows // BLOCK) <= 16

    def piece_at(k):
        return pl.BlockSpec(
            (rows, cols), lambda i, me: (0, lax.rem(me[0] + k, pieces) * kv_heads + head)
        )

    in_specs = [piece_at(k) for k in range(pieces)] * 2
    for array in ends:
        last = array.shape[1] // W - 1
        in_specs += [pl.BlockSpec((ends_of, W, array.shape[2]), lambda i, me: (0, last, 0))]
    in_specs += [pl.BlockSpec(memory_space=pl.ANY)]
    operands = [cotan] * pieces + [output] * pieces + [*ends, after]
    out_specs = [pl.BlockSpec((rows + 16, cols), lambda i, me: (0, 0))] * pieces
    out_shape = [jax.ShapeDtypeStruct((rows + 16, cols), BF16)] * pieces
    if ends:
        shape = (len(ends), ends_of, W, ends[0].shape[2])
        out_specs += [pl.BlockSpec(shape, lambda i, me: (0, 0, 0, 0))]
        out_shape += [jax.ShapeDtypeStruct(shape, BF16)]
    scratch = [pltpu.VMEM((16, cols), F32)]
    return pl.pallas_call(
        functools.partial(pack_kernel, pieces, len(ends)),
        grid_spec=pltpu.PrefetchScalarGridSpec(
            num_scalar_prefetch=1,
            grid=(1,),
            in_specs=in_specs,
            out_specs=out_specs,
            scratch_shapes=scratch,
        ),
        out_shape=out_shape,
        compiler_params=pltpu.CompilerParams(vmem_limit_bytes=VMEM_LIMIT),
        cost_estimate=pl.CostEstimate(
            flops=4 * rows * cols * pieces, bytes_accessed=6 * rows * cols * pieces, transcendentals=0
        ),
        name="pack_cotangent",
    )(me, *operands)


def rim_kernel(key_ref, value_ref, after_ref, out_ref):
    out_ref[0] = key_ref[...]
    out_ref[1] = value_ref[...]


def rim_call(keys, values, from_head, after):
    kv_heads, tok_rows, head_dim = keys.shape
    last = pl.BlockSpec((1, W, head_dim), lambda i: (i + from_head, tok_rows // W - 1, 0))
    return pl.pallas_call(
        rim_kernel,
        grid=(kv_heads - from_head,),
        in_specs=[last, last, pl.BlockSpec(memory_space=pl.ANY)],
        out_specs=pl.BlockSpec((2, 1, W, head_dim), lambda i: (0, i, 0, 0)),
        out_shape=jax.ShapeDtypeStruct((2, kv_heads - from_head, W, head_dim), BF16),
        name="rims",
    )(keys, values, after)


def head_kernel(head, window, tok_rows, blocks, carried, aliased, passed, me_ref, *refs):
    q_ref, kh_ref, ko_ref, vh_ref, vo_ref, lse_ref, start_ref = refs[:7]
    groups, _, head_dim = q_ref.shape
    first_block, count = blocks
    opening = first_block == 0
    closing = first_block + count == tok_rows // BLOCK
    outputs = 1 + (4 if closing else 2) + opening
    pieces = len(refs) - 7 - 2 * carried - aliased - 2 * passed - outputs - 8
    cotan_refs = refs[7 : 7 + pieces]
    refs = refs[7 + pieces :]
    carry_refs = refs[: 2 * carried]
    refs = refs[2 * carried + aliased + passed :]
    dq_ref = refs[0]
    k_all, v_all, kt_all, cotan_all, delta_all, ds_all, dk_all, dv_all = refs[outputs + passed :]
    piece_rows = tok_rows // pieces
    in_piece = piece_rows // BLOCK
    span = window + BLOCK
    cols = groups * BLOCK
    scale = QPRE ** (-0.5)
    me = me_ref[0]
    base = first_block * BLOCK
    extent = k_all.shape[0]
    in_rim = max(window - base, 0)

    for all_ref, rim_ref, own_ref in ((k_all, kh_ref, ko_ref), (v_all, vh_ref, vo_ref)):
        if in_rim:
            all_ref[:in_rim] = rim_ref[base:]
        skip = base + in_rim - window
        all_ref[in_rim:] = own_ref[0, skip : skip + extent - in_rim]
    unit = (
        lax.broadcasted_iota(jnp.int32, (head_dim, head_dim), 0)
        == lax.broadcasted_iota(jnp.int32, (head_dim, head_dim), 1)
    ).astype(BF16)
    kt_all[...] = lax.dot_general(unit, k_all[...], NT, preferred_element_type=F32).astype(BF16)
    dk_all[...] = jnp.zeros_like(dk_all)
    dv_all[...] = jnp.zeros_like(dv_all)
    for all_ref, carry_ref in zip((dk_all, dv_all), carry_refs):
        all_ref[: carry_ref.shape[0]] = carry_ref[...]
    ds_all[ds_all.shape[0] - 1] = jnp.zeros(ds_all.shape[1:], BF16)
    for i in range(pieces):
        source = lax.rem(me - i + pieces, pieces)
        where = pl.ds(pl.multiple_of(source * piece_rows, piece_rows), piece_rows)
        for j in range(groups):
            cotan_all[j, where, :] = cotan_refs[i][:piece_rows, j * head_dim : (j + 1) * head_dim]
        parts = cotan_refs[i][piece_rows:].astype(F32)
        for j in range(in_piece):
            row = parts[j : j + 1] + parts[in_piece + j : in_piece + j + 1]
            delta_all[source * in_piece + j] = row + parts[2 * in_piece + j : 2 * in_piece + j + 1]

    def write_query(first, slot):
        dq = lax.dot_general(
            kt_all[:, pl.ds(first, span)], ds_all[slot], NN, preferred_element_type=F32
        )
        dq = (dq.T * F32(scale)).astype(BF16)
        dq_ref[:, pl.ds(first, BLOCK), :] = dq.reshape(groups, BLOCK, head_dim)

    token = lax.broadcasted_iota(jnp.int32, (1, cols), 1) % BLOCK
    place = lax.broadcasted_iota(jnp.int32, (SUB, cols), 0)
    chunks = span // BLOCK
    unroll = ds_all.shape[0]

    def load(index):
        first = pl.multiple_of(index * BLOCK, BLOCK)
        token_first = pl.multiple_of(base + first, BLOCK)
        here = pl.ds(token_first, BLOCK)
        query = q_ref[:, pl.ds(first, BLOCK), :].reshape(cols, head_dim)
        cotan = cotan_all[:, here, :].reshape(cols, head_dim)
        rows = [lse_ref[head * groups + i : head * groups + i + 1, here] for i in range(groups)]
        lse = jnp.concatenate(rows, axis=1) * F32(LOG2E)
        delta = delta_all[first_block + index]
        start = jnp.concatenate([start_ref[:, here]] * groups, axis=1) - token_first
        lower = jnp.maximum(start, token + 1)
        return first, query, cotan, lse, delta, lower

    def span_of(first, i):
        return pl.ds(pl.multiple_of(first + i * BLOCK, BLOCK), BLOCK)

    def front(block, i):
        first, query, cotan = block[:3]
        rows = span_of(first, i)
        return (
            lax.dot_general(k_all[rows, :], query, NT, preferred_element_type=F32),
            lax.dot_general(v_all[rows, :], cotan, NT, preferred_element_type=F32),
        )

    def back(block, i, probs_low, dscores):
        first, query, cotan = block[:3]
        rows = span_of(first, i)
        dv_all[rows, :] += lax.dot_general(probs_low, cotan, NN, preferred_element_type=F32)
        dk_all[rows, :] += lax.dot_general(dscores, query, NN, preferred_element_type=F32)

    def middle(block, slot, i, scores, dprobs):
        _, _, _, lse, delta, lower = block
        lows = []
        for at in range(0, BLOCK, SUB):
            part = slice(at, at + SUB)
            shift = i * BLOCK + at
            allowed = place >= lower - shift
            if shift + SUB > window:
                allowed = allowed & (place <= token + (window - shift))
            probs = jnp.where(
                allowed, jnp.exp2(scores[part] * F32(scale * LOG2E) - lse), F32(0.0)
            )
            dscores = (probs * (dprobs[part] - delta)).astype(BF16)
            ds_all[slot, shift : shift + SUB, :] = dscores
            lows.append((probs.astype(BF16), dscores))
        probs_low = jnp.concatenate([x for x, _ in lows], axis=0)
        dscores = jnp.concatenate([x for _, x in lows], axis=0)
        return probs_low, dscores

    def some_blocks(index, nothing):
        blocks = [load(unroll * index + j) for j in range(unroll)]
        stages = [(j, i) for j in range(unroll) for i in range(chunks)]
        ready = front(blocks[0], 0)
        before = jnp.maximum(unroll * index - 1, 0)
        write_query(pl.multiple_of(before * BLOCK, BLOCK), unroll - 1)
        held = None
        for n, (j, i) in enumerate(stages):
            scores, dprobs = ready
            if n + 1 < len(stages):
                jj, ii = stages[n + 1]
                ready = front(blocks[jj], ii)
            if held is not None:
                back(*held)
            if i == 1 and j > 0:
                write_query(blocks[j - 1][0], j - 1)
            held = (blocks[j], i, *middle(blocks[j], j, i, scores, dprobs))
        back(*held)
        return nothing

    lax.fori_loop(0, count // unroll, some_blocks, 0)
    write_query((count - 1) * BLOCK, unroll - 1)

    if closing:
        dk_ref, dv_ref, dk_tail_ref, dv_tail_ref = refs[1:5]
        tail = extent - window
        own = tail - dk_ref.shape[1]
        dk_ref[0] = (dk_all[own:tail] * F32(scale)).astype(BF16)
        dv_ref[0] = dv_all[own:tail].astype(BF16)
        dk_tail_ref[0] = (dk_all[tail:] * F32(scale)).astype(BF16)
        dv_tail_ref[0] = dv_all[tail:].astype(BF16)
    else:
        dk_next_ref, dv_next_ref = refs[1:3]
        dk_next_ref[...] = dk_all[extent - window :]
        dv_next_ref[...] = dv_all[extent - window :]
    if opening:
        halo_ref = refs[outputs - 1]
        halo_ref[0, 0] = (dk_all[:window] * F32(scale)).astype(BF16)
        halo_ref[0, 1] = dv_all[:window].astype(BF16)


def head_call(
    head, blocks, me, queries, rims, rim_head, keys, values, lse, start, cotans, before, carry, passing, halo=None
):
    kv_heads, tok_rows, head_dim = keys.shape
    q_heads = queries.shape[0]
    groups = q_heads // kv_heads
    window = rims.shape[2]
    pieces = len(cotans)
    own = tok_rows - window
    first_block, count = blocks
    assert first_block % count == 0
    extent = count * BLOCK + window
    rim_rows = window if first_block == 0 else BLOCK
    own_rows = min(first_block * BLOCK + extent - window, tok_rows)

    def at_head(*block):
        return pl.BlockSpec(block, lambda i, me: (head, 0, 0))

    def full(*block):
        return pl.BlockSpec(block, lambda i, me: (0,) * len(block))

    q_spec = pl.BlockSpec(
        (groups, count * BLOCK, head_dim), lambda i, me: (head, first_block // count, 0)
    )
    in_specs = [
        q_spec,
        pl.BlockSpec((None, None, rim_rows, head_dim), lambda i, me: (0, rim_head, 0, 0)),
        at_head(1, own_rows, head_dim),
        pl.BlockSpec((None, None, rim_rows, head_dim), lambda i, me: (1, rim_head, 0, 0)),
        at_head(1, own_rows, head_dim),
        full(q_heads, tok_rows),
        full(1, tok_rows),
    ]
    in_specs += [full(*cotans[0].shape)] * pieces
    in_specs += [full(*array.shape) for array in carry]
    n_in = 1 + 7 + pieces + len(carry)
    aliases = {n_in + i: i for i in range(len(before))}
    unroll = math.gcd(UNROLL, count)
    out_specs = [q_spec]
    out_shape = [jax.ShapeDtypeStruct(queries.shape, BF16)]
    if first_block + count == tok_rows // BLOCK:
        out_specs += [at_head(1, own, head_dim)] * 2 + [at_head(1, window, head_dim)] * 2
        out_shape += [jax.ShapeDtypeStruct(keys.shape, BF16)] * 2
        out_shape += [jax.ShapeDtypeStruct((kv_heads, window, head_dim), BF16)] * 2
    else:
        out_specs += [full(window, head_dim)] * 2
        out_shape += [jax.ShapeDtypeStruct((window, head_dim), F32)] * 2
    if first_block == 0:
        slot, size, earlier = halo
        out_specs += [pl.BlockSpec((1, 2, window, head_dim), lambda i, me: (slot, 0, 0, 0))]
        out_shape += [jax.ShapeDtypeStruct((size, 2, window, head_dim), BF16)]
        if earlier is not None:
            aliases[n_in + len(before)] = len(out_shape) - 1
            before = [*before, earlier]
    scratch = [
        pltpu.VMEM((extent, head_dim), BF16),
        pltpu.VMEM((extent, head_dim), BF16),
        pltpu.VMEM((head_dim, extent), BF16),
        pltpu.VMEM((groups, tok_rows, head_dim), BF16),
        pltpu.VMEM((tok_rows // BLOCK, 1, groups * BLOCK), F32),
        pltpu.VMEM((unroll, window + BLOCK, groups * BLOCK), BF16),
        pltpu.VMEM((extent, head_dim), F32),
        pltpu.VMEM((extent, head_dim), F32),
    ]
    in_specs += [pl.BlockSpec(memory_space=pl.ANY)] * (len(before) + len(passing))
    for i, array in enumerate(passing):
        aliases[n_in + len(before) + i] = len(out_shape)
        out_shape.append(jax.ShapeDtypeStruct(array.shape, array.dtype))
        out_specs.append(pl.BlockSpec(memory_space=pl.ANY))
    pairs = groups * count * BLOCK * (window + BLOCK)
    return pl.pallas_call(
        functools.partial(
            head_kernel, head, window, tok_rows, blocks, len(carry) // 2, len(before), len(passing)
        ),
        grid_spec=pltpu.PrefetchScalarGridSpec(
            num_scalar_prefetch=1,
            grid=(1,),
            in_specs=in_specs,
            out_specs=out_specs,
            scratch_shapes=scratch,
        ),
        out_shape=out_shape,
        input_output_aliases=aliases,
        compiler_params=pltpu.CompilerParams(vmem_limit_bytes=VMEM_LIMIT),
        cost_estimate=pl.CostEstimate(
            flops=40 * pairs * head_dim, bytes_accessed=8 * tok_rows, transcendentals=0
        ),
        name="head_backward",
    )(me, queries, rims, keys, rims, values, lse, start, *cotans, *carry, *before, *passing)


def join_kernel(joint, dk_tail_ref, dv_tail_ref, *refs):
    backs = refs[:-4]
    dk_ref, dv_ref = refs[-2:]

    def join(back_ref):
        dk_ref[...] = (dk_tail_ref[...].astype(F32) + back_ref[:, 0].astype(F32)).astype(BF16)
        dv_ref[...] = (dv_tail_ref[...].astype(F32) + back_ref[:, 1].astype(F32)).astype(BF16)

    if len(backs) == 1:
        join(backs[0])
    else:
        pl.when(pl.program_id(0) < joint)(lambda: join(backs[0]))
        pl.when(pl.program_id(0) >= joint)(lambda: join(backs[1]))


def join_call(dk_tail, dv_tail, backs, grad_keys, grad_values):
    kv_heads, window, head_dim = dk_tail.shape
    last = grad_keys.shape[1] // window - 1
    joint = backs[0].shape[0]
    tail = pl.BlockSpec((1, window, head_dim), lambda i: (i, 0, 0))
    out = pl.BlockSpec((1, window, head_dim), lambda i: (i, last, 0))
    anywhere = pl.BlockSpec(memory_space=pl.ANY)
    shape = (1, 2, window, head_dim)
    back_specs = [pl.BlockSpec(shape, lambda i: (jnp.minimum(i, joint - 1), 0, 0, 0))]
    back_specs += [pl.BlockSpec(shape, lambda i: (0, 0, 0, 0))] * (len(backs) - 1)
    return pl.pallas_call(
        functools.partial(join_kernel, joint),
        grid=(kv_heads,),
        in_specs=[tail, tail, *back_specs, anywhere, anywhere],
        out_specs=[out, out],
        out_shape=[jax.ShapeDtypeStruct(grad_keys.shape, BF16)] * 2,
        input_output_aliases={2 + len(backs): 0, 3 + len(backs): 1},
        compiler_params=pltpu.CompilerParams(vmem_limit_bytes=VMEM_LIMIT),
        name="join_tails",
    )(dk_tail, dv_tail, *backs, grad_keys, grad_values)


def body(queries, key_states, value_states, attn_output, out_cotangent, logsumexp, doc_start):
    kv_heads, tok_rows, head_dim = key_states.shape
    groups = queries.shape[0] // kv_heads
    pieces = lax.axis_size("head")
    me = lax.axis_index("head").astype(jnp.int32)[None]
    start = doc_start[None, :] - lax.axis_index("ctx") * tok_rows + W
    steps = tok_rows // BLOCK

    def sent(block, distance):
        route = [(i, (i + distance) % pieces) for i in range(pieces)]
        return lax.ppermute(block, "head", route)

    def packed(head, after, *ends):
        return pack_call(
            head, me, out_cotangent, attn_output, kv_heads, groups * head_dim, pieces, after, *ends
        )

    def arrived(parts):
        return [part if k == 0 else sent(part, k) for k, part in enumerate(parts)]

    early = (kv_heads + 1) // 2
    *first, ends = packed(0, out_cotangent, (key_states, value_states), early)
    parts = {0: first}
    cotans = {0: arrived(first)}
    rims = [from_behind(ends, "ctx", 1)]
    after = first[0]
    for head in range(kv_heads - 1, 0, -1):
        parts[head] = packed(head, after)
        after = parts[head][0]
    if kv_heads > 1:
        held = lax.optimization_barrier((*parts[1], *cotans[0][1:]))
        parts[1], cotans[0][1:] = list(held[:pieces]), held[pieces:]
        cotans[1] = arrived(parts[1])
    if kv_heads > early:
        ends = rim_call(key_states, value_states, early, after)
        rims.append(from_behind(ends, "ctx", 1))

    split = 2 * W == tok_rows
    final = kv_heads - 1 if split else kv_heads
    before = []
    halos = None
    backs = []
    for head in range(kv_heads):
        later = parts[head + 2] if head + 2 < kv_heads else []
        halo = (head, final, halos) if head < final else (0, 1, None)
        call = functools.partial(
            head_call, head, me=me, queries=queries, rims=rims[int(head >= early)],
            rim_head=head - early * (head >= early), keys=key_states, values=value_states,
            lse=logsumexp, start=start, cotans=cotans[head], halo=halo,
        )
        if head + 1 < kv_heads or not split:
            got = call((0, steps), before=before, carry=[], passing=later[1:])
            if later:
                middle = pieces // 2
                moving = list(got[6:])
                held = lax.optimization_barrier((moving[middle - 1], *cotans[head + 1][1:]))
                moving[middle - 1] = held[0]
                cotans[head + 1][1:] = held[1:]
                cotans[head + 2] = arrived([later[0], *moving])
            before, halos = list(got[:5]), got[5]
        else:
            got = call((0, steps // 2), before=before[:1], carry=[], passing=[])
            halos = got[3]
        if head >= final - 1:
            backs.append(from_behind(halos, "ctx", -1))
        if head + 1 == kv_heads and split:
            before = call(
                (steps // 2, steps // 2), before=[got[0], *before[1:]], carry=got[1:3], passing=[]
            )
    grad_queries, grad_keys, grad_values, *tails = before
    grad_keys, grad_values = join_call(*tails, backs, grad_keys, grad_values)
    return grad_queries, grad_keys, grad_values


def solution(mesh):
    return jax.shard_map(
        body,
        mesh=mesh,
        in_specs=(
            P("head", "ctx", None),
            P("head", "ctx", None),
            P("head", "ctx", None),
            P(("ctx", "head"), None),
            P(("ctx", "head"), None),
            P("head", "ctx"),
            P("ctx"),
        ),
        out_specs=(P("head", "ctx", None), P("head", "ctx", None), P("head", "ctx", None)),
        check_vma=False,
    )
```

```python
import functools
import math

import jax
import jax.numpy as jnp
from jax import lax
from jax.experimental import pallas as pl
from jax.experimental.pallas import tpu as pltpu
from jax.sharding import PartitionSpec as P

W = 1024
QPRE = 168
BLOCK = 128
SUB = 32
UNROLL = 4
VMEM_LIMIT = 64 * 1024 * 1024 - 131072
LOG2E = math.log2(math.e)
F32 = jnp.float32
BF16 = jnp.bfloat16
NT = (((1,), (1,)), ((), ()))
NN = (((1,), (0,)), ((), ()))


def from_behind(block, axis, distance):
    devices = range(lax.axis_size(axis))
    route = [(i - distance, i) for i in devices if i - distance in devices]
    return lax.ppermute(block, axis, route)


def pack_kernel(pieces, ends, me_ref, *refs):
    cotan_refs, output_refs = refs[:pieces], refs[pieces : 2 * pieces]
    end_refs = refs[2 * pieces : 2 * pieces + ends]
    refs = refs[2 * pieces + ends + 1 :]
    out_refs, rows_ref = refs[:pieces], refs[-1]
    for i in range(ends):
        refs[pieces][i] = end_refs[i][...]
    rows, cols = cotan_refs[0].shape
    groups = cols // BLOCK
    in_piece = rows // BLOCK
    head_of = lax.broadcasted_iota(jnp.int32, (16, cols), 1) // BLOCK
    member = (head_of == lax.broadcasted_iota(jnp.int32, (16, cols), 0)).astype(BF16)
    rows_ref[...] = jnp.zeros_like(rows_ref)
    for k in range(pieces):
        cotan = cotan_refs[k][...]
        product = cotan.astype(F32) * output_refs[k][...].astype(F32)
        high = product.astype(BF16)
        low = (product - high.astype(F32)).astype(BF16)
        delta = lax.dot_general(member, high, NT, preferred_element_type=F32)
        delta = delta + lax.dot_general(member, low, NT, preferred_element_type=F32)
        out_refs[k][:rows] = cotan
        for part in range(3):
            rounded = delta.astype(BF16).astype(F32)
            delta = delta - rounded
            for j in range(in_piece):
                for i in range(groups):
                    rows_ref[
                        part * in_piece + j : part * in_piece + j + 1, i * BLOCK : (i + 1) * BLOCK
                    ] = rounded[i : i + 1, j * BLOCK : (j + 1) * BLOCK]
        out_refs[k][rows:] = rows_ref[...].astype(BF16)


def pack_call(head, me, cotan, output, kv_heads, cols, pieces, after, ends=(), ends_of=0):
    rows = cotan.shape[0]
    assert 3 * (rows // BLOCK) <= 16

    def piece_at(k):
        return pl.BlockSpec(
            (rows, cols), lambda i, me: (0, lax.rem(me[0] + k, pieces) * kv_heads + head)
        )

    in_specs = [piece_at(k) for k in range(pieces)] * 2
    for array in ends:
        last = array.shape[1] // W - 1
        in_specs += [pl.BlockSpec((ends_of, W, array.shape[2]), lambda i, me: (0, last, 0))]
    in_specs += [pl.BlockSpec(memory_space=pl.ANY)]
    operands = [cotan] * pieces + [output] * pieces + [*ends, after]
    out_specs = [pl.BlockSpec((rows + 16, cols), lambda i, me: (0, 0))] * pieces
    out_shape = [jax.ShapeDtypeStruct((rows + 16, cols), BF16)] * pieces
    if ends:
        shape = (len(ends), ends_of, W, ends[0].shape[2])
        out_specs += [pl.BlockSpec(shape, lambda i, me: (0, 0, 0, 0))]
        out_shape += [jax.ShapeDtypeStruct(shape, BF16)]
    scratch = [pltpu.VMEM((16, cols), F32)]
    return pl.pallas_call(
        functools.partial(pack_kernel, pieces, len(ends)),
        grid_spec=pltpu.PrefetchScalarGridSpec(
            num_scalar_prefetch=1,
            grid=(1,),
            in_specs=in_specs,
            out_specs=out_specs,
            scratch_shapes=scratch,
        ),
        out_shape=out_shape,
        compiler_params=pltpu.CompilerParams(vmem_limit_bytes=VMEM_LIMIT),
        cost_estimate=pl.CostEstimate(
            flops=4 * rows * cols * pieces, bytes_accessed=6 * rows * cols * pieces, transcendentals=0
        ),
        name="pack_cotangent",
    )(me, *operands)


def rim_kernel(key_ref, value_ref, after_ref, out_ref):
    out_ref[0] = key_ref[...]
    out_ref[1] = value_ref[...]


def rim_call(keys, values, from_head, after):
    kv_heads, tok_rows, head_dim = keys.shape
    last = pl.BlockSpec((1, W, head_dim), lambda i: (i + from_head, tok_rows // W - 1, 0))
    return pl.pallas_call(
        rim_kernel,
        grid=(kv_heads - from_head,),
        in_specs=[last, last, pl.BlockSpec(memory_space=pl.ANY)],
        out_specs=pl.BlockSpec((2, 1, W, head_dim), lambda i: (0, i, 0, 0)),
        out_shape=jax.ShapeDtypeStruct((2, kv_heads - from_head, W, head_dim), BF16),
        name="rims",
    )(keys, values, after)


def head_kernel(head, window, tok_rows, blocks, carried, aliased, passed, me_ref, *refs):
    q_ref, kh_ref, ko_ref, vh_ref, vo_ref, lse_ref, start_ref = refs[:7]
    groups, _, head_dim = q_ref.shape
    first_block, count = blocks
    opening = first_block == 0
    closing = first_block + count == tok_rows // BLOCK
    outputs = 1 + (4 if closing else 2) + opening
    pieces = len(refs) - 7 - 2 * carried - aliased - 2 * passed - outputs - 8
    cotan_refs = refs[7 : 7 + pieces]
    refs = refs[7 + pieces :]
    carry_refs = refs[: 2 * carried]
    refs = refs[2 * carried + aliased + passed :]
    dq_ref = refs[0]
    k_all, v_all, kt_all, cotan_all, delta_all, ds_all, dk_all, dv_all = refs[outputs + passed :]
    piece_rows = tok_rows // pieces
    in_piece = piece_rows // BLOCK
    span = window + BLOCK
    cols = groups * BLOCK
    scale = QPRE ** (-0.5)
    me = me_ref[0]
    base = first_block * BLOCK
    extent = k_all.shape[0]
    in_rim = max(window - base, 0)

    for all_ref, rim_ref, own_ref in ((k_all, kh_ref, ko_ref), (v_all, vh_ref, vo_ref)):
        if in_rim:
            all_ref[:in_rim] = rim_ref[base:]
        skip = base + in_rim - window
        all_ref[in_rim:] = own_ref[0, skip : skip + extent - in_rim]
    unit = (
        lax.broadcasted_iota(jnp.int32, (head_dim, head_dim), 0)
        == lax.broadcasted_iota(jnp.int32, (head_dim, head_dim), 1)
    ).astype(BF16)
    kt_all[...] = lax.dot_general(unit, k_all[...], NT, preferred_element_type=F32).astype(BF16)
    dk_all[...] = jnp.zeros_like(dk_all)
    dv_all[...] = jnp.zeros_like(dv_all)
    for all_ref, carry_ref in zip((dk_all, dv_all), carry_refs):
        all_ref[: carry_ref.shape[0]] = carry_ref[...]
    ds_all[ds_all.shape[0] - 1] = jnp.zeros(ds_all.shape[1:], BF16)
    for i in range(pieces):
        source = lax.rem(me - i + pieces, pieces)
        where = pl.ds(pl.multiple_of(source * piece_rows, piece_rows), piece_rows)
        for j in range(groups):
            cotan_all[j, where, :] = cotan_refs[i][:piece_rows, j * head_dim : (j + 1) * head_dim]
        parts = cotan_refs[i][piece_rows:].astype(F32)
        for j in range(in_piece):
            row = parts[j : j + 1] + parts[in_piece + j : in_piece + j + 1]
            delta_all[source * in_piece + j] = row + parts[2 * in_piece + j : 2 * in_piece + j + 1]

    def write_query(first, slot):
        dq = lax.dot_general(
            kt_all[:, pl.ds(first, span)], ds_all[slot], NN, preferred_element_type=F32
        )
        dq = (dq.T * F32(scale)).astype(BF16)
        dq_ref[:, pl.ds(first, BLOCK), :] = dq.reshape(groups, BLOCK, head_dim)

    token = lax.broadcasted_iota(jnp.int32, (1, cols), 1) % BLOCK
    place = lax.broadcasted_iota(jnp.int32, (SUB, cols), 0)
    chunks = span // BLOCK
    unroll = ds_all.shape[0]

    def load(index):
        first = pl.multiple_of(index * BLOCK, BLOCK)
        token_first = pl.multiple_of(base + first, BLOCK)
        here = pl.ds(token_first, BLOCK)
        query = q_ref[:, pl.ds(first, BLOCK), :].reshape(cols, head_dim)
        cotan = cotan_all[:, here, :].reshape(cols, head_dim)
        rows = [lse_ref[head * groups + i : head * groups + i + 1, here] for i in range(groups)]
        lse = jnp.concatenate(rows, axis=1) * F32(LOG2E)
        delta = delta_all[first_block + index]
        start = jnp.concatenate([start_ref[:, here]] * groups, axis=1) - token_first
        lower = jnp.maximum(start, token + 1)
        return first, query, cotan, lse, delta, lower

    def span_of(first, i):
        return pl.ds(pl.multiple_of(first + i * BLOCK, BLOCK), BLOCK)

    def front(block, i):
        first, query, cotan = block[:3]
        rows = span_of(first, i)
        return (
            lax.dot_general(k_all[rows, :], query, NT, preferred_element_type=F32),
            lax.dot_general(v_all[rows, :], cotan, NT, preferred_element_type=F32),
        )

    def back(block, i, probs_low, dscores):
        first, query, cotan = block[:3]
        rows = span_of(first, i)
        dv_all[rows, :] += lax.dot_general(probs_low, cotan, NN, preferred_element_type=F32)
        dk_all[rows, :] += lax.dot_general(dscores, query, NN, preferred_element_type=F32)

    def middle(block, slot, i, scores, dprobs):
        _, _, _, lse, delta, lower = block
        lows = []
        for at in range(0, BLOCK, SUB):
            part = slice(at, at + SUB)
            shift = i * BLOCK + at
            allowed = place >= lower - shift
            if shift + SUB > window:
                allowed = allowed & (place <= token + (window - shift))
            probs = jnp.where(
                allowed, jnp.exp2(scores[part] * F32(scale * LOG2E) - lse), F32(0.0)
            )
            dscores = (probs * (dprobs[part] - delta)).astype(BF16)
            ds_all[slot, shift : shift + SUB, :] = dscores
            lows.append((probs.astype(BF16), dscores))
        probs_low = jnp.concatenate([x for x, _ in lows], axis=0)
        dscores = jnp.concatenate([x for _, x in lows], axis=0)
        return probs_low, dscores

    def some_blocks(index, nothing):
        blocks = [load(unroll * index + j) for j in range(unroll)]
        stages = [(j, i) for j in range(unroll) for i in range(chunks)]
        ready = front(blocks[0], 0)
        before = jnp.maximum(unroll * index - 1, 0)
        write_query(pl.multiple_of(before * BLOCK, BLOCK), unroll - 1)
        held = None
        for n, (j, i) in enumerate(stages):
            scores, dprobs = ready
            if n + 1 < len(stages):
                jj, ii = stages[n + 1]
                ready = front(blocks[jj], ii)
            if held is not None:
                back(*held)
            if i == 1 and j > 0:
                write_query(blocks[j - 1][0], j - 1)
            held = (blocks[j], i, *middle(blocks[j], j, i, scores, dprobs))
        back(*held)
        return nothing

    lax.fori_loop(0, count // unroll, some_blocks, 0)
    write_query((count - 1) * BLOCK, unroll - 1)

    if closing:
        dk_ref, dv_ref, dk_tail_ref, dv_tail_ref = refs[1:5]
        tail = extent - window
        own = tail - dk_ref.shape[1]
        dk_ref[0] = (dk_all[own:tail] * F32(scale)).astype(BF16)
        dv_ref[0] = dv_all[own:tail].astype(BF16)
        dk_tail_ref[0] = (dk_all[tail:] * F32(scale)).astype(BF16)
        dv_tail_ref[0] = dv_all[tail:].astype(BF16)
    else:
        dk_next_ref, dv_next_ref = refs[1:3]
        dk_next_ref[...] = dk_all[extent - window :]
        dv_next_ref[...] = dv_all[extent - window :]
    if opening:
        halo_ref = refs[outputs - 1]
        halo_ref[0, 0] = (dk_all[:window] * F32(scale)).astype(BF16)
        halo_ref[0, 1] = dv_all[:window].astype(BF16)


def head_call(
    head, blocks, me, queries, rims, rim_head, keys, values, lse, start, cotans, before, carry, passing, halo=None
):
    kv_heads, tok_rows, head_dim = keys.shape
    q_heads = queries.shape[0]
    groups = q_heads // kv_heads
    window = rims.shape[2]
    pieces = len(cotans)
    own = tok_rows - window
    first_block, count = blocks
    assert first_block % count == 0
    extent = count * BLOCK + window
    rim_rows = window if first_block == 0 else BLOCK
    own_rows = min(first_block * BLOCK + extent - window, tok_rows)

    def at_head(*block):
        return pl.BlockSpec(block, lambda i, me: (head, 0, 0))

    def full(*block):
        return pl.BlockSpec(block, lambda i, me: (0,) * len(block))

    q_spec = pl.BlockSpec(
        (groups, count * BLOCK, head_dim), lambda i, me: (head, first_block // count, 0)
    )
    in_specs = [
        q_spec,
        pl.BlockSpec((None, None, rim_rows, head_dim), lambda i, me: (0, rim_head, 0, 0)),
        at_head(1, own_rows, head_dim),
        pl.BlockSpec((None, None, rim_rows, head_dim), lambda i, me: (1, rim_head, 0, 0)),
        at_head(1, own_rows, head_dim),
        full(q_heads, tok_rows),
        full(1, tok_rows),
    ]
    in_specs += [full(*cotans[0].shape)] * pieces
    in_specs += [full(*array.shape) for array in carry]
    n_in = 1 + 7 + pieces + len(carry)
    aliases = {n_in + i: i for i in range(len(before))}
    unroll = count if count <= 2 * UNROLL else math.gcd(UNROLL, count)
    out_specs = [q_spec]
    out_shape = [jax.ShapeDtypeStruct(queries.shape, BF16)]
    if first_block + count == tok_rows // BLOCK:
        out_specs += [at_head(1, own, head_dim)] * 2 + [at_head(1, window, head_dim)] * 2
        out_shape += [jax.ShapeDtypeStruct(keys.shape, BF16)] * 2
        out_shape += [jax.ShapeDtypeStruct((kv_heads, window, head_dim), BF16)] * 2
    else:
        out_specs += [full(window, head_dim)] * 2
        out_shape += [jax.ShapeDtypeStruct((window, head_dim), F32)] * 2
    if first_block == 0:
        slot, size, earlier = halo
        out_specs += [pl.BlockSpec((1, 2, window, head_dim), lambda i, me: (slot, 0, 0, 0))]
        out_shape += [jax.ShapeDtypeStruct((size, 2, window, head_dim), BF16)]
        if earlier is not None:
            aliases[n_in + len(before)] = len(out_shape) - 1
            before = [*before, earlier]
    scratch = [
        pltpu.VMEM((extent, head_dim), BF16),
        pltpu.VMEM((extent, head_dim), BF16),
        pltpu.VMEM((head_dim, extent), BF16),
        pltpu.VMEM((groups, tok_rows, head_dim), BF16),
        pltpu.VMEM((tok_rows // BLOCK, 1, groups * BLOCK), F32),
        pltpu.VMEM((unroll, window + BLOCK, groups * BLOCK), BF16),
        pltpu.VMEM((extent, head_dim), F32),
        pltpu.VMEM((extent, head_dim), F32),
    ]
    in_specs += [pl.BlockSpec(memory_space=pl.ANY)] * (len(before) + len(passing))
    for i, array in enumerate(passing):
        aliases[n_in + len(before) + i] = len(out_shape)
        out_shape.append(jax.ShapeDtypeStruct(array.shape, array.dtype))
        out_specs.append(pl.BlockSpec(memory_space=pl.ANY))
    pairs = groups * count * BLOCK * (window + BLOCK)
    return pl.pallas_call(
        functools.partial(
            head_kernel, head, window, tok_rows, blocks, len(carry) // 2, len(before), len(passing)
        ),
        grid_spec=pltpu.PrefetchScalarGridSpec(
            num_scalar_prefetch=1,
            grid=(1,),
            in_specs=in_specs,
            out_specs=out_specs,
            scratch_shapes=scratch,
        ),
        out_shape=out_shape,
        input_output_aliases=aliases,
        compiler_params=pltpu.CompilerParams(vmem_limit_bytes=VMEM_LIMIT),
        cost_estimate=pl.CostEstimate(
            flops=40 * pairs * head_dim, bytes_accessed=8 * tok_rows, transcendentals=0
        ),
        name="head_backward",
    )(me, queries, rims, keys, rims, values, lse, start, *cotans, *carry, *before, *passing)


def join_kernel(joint, dk_tail_ref, dv_tail_ref, *refs):
    backs = refs[:-4]
    dk_ref, dv_ref = refs[-2:]

    def join(back_ref):
        dk_ref[...] = (dk_tail_ref[...].astype(F32) + back_ref[:, 0].astype(F32)).astype(BF16)
        dv_ref[...] = (dv_tail_ref[...].astype(F32) + back_ref[:, 1].astype(F32)).astype(BF16)

    if len(backs) == 1:
        join(backs[0])
    else:
        pl.when(pl.program_id(0) < joint)(lambda: join(backs[0]))
        pl.when(pl.program_id(0) >= joint)(lambda: join(backs[1]))


def join_call(dk_tail, dv_tail, backs, grad_keys, grad_values):
    kv_heads, window, head_dim = dk_tail.shape
    last = grad_keys.shape[1] // window - 1
    joint = backs[0].shape[0]
    tail = pl.BlockSpec((1, window, head_dim), lambda i: (i, 0, 0))
    out = pl.BlockSpec((1, window, head_dim), lambda i: (i, last, 0))
    anywhere = pl.BlockSpec(memory_space=pl.ANY)
    shape = (1, 2, window, head_dim)
    back_specs = [pl.BlockSpec(shape, lambda i: (jnp.minimum(i, joint - 1), 0, 0, 0))]
    back_specs += [pl.BlockSpec(shape, lambda i: (0, 0, 0, 0))] * (len(backs) - 1)
    return pl.pallas_call(
        functools.partial(join_kernel, joint),
        grid=(kv_heads,),
        in_specs=[tail, tail, *back_specs, anywhere, anywhere],
        out_specs=[out, out],
        out_shape=[jax.ShapeDtypeStruct(grad_keys.shape, BF16)] * 2,
        input_output_aliases={2 + len(backs): 0, 3 + len(backs): 1},
        compiler_params=pltpu.CompilerParams(vmem_limit_bytes=VMEM_LIMIT),
        name="join_tails",
    )(dk_tail, dv_tail, *backs, grad_keys, grad_values)


def body(queries, key_states, value_states, attn_output, out_cotangent, logsumexp, doc_start):
    kv_heads, tok_rows, head_dim = key_states.shape
    groups = queries.shape[0] // kv_heads
    pieces = lax.axis_size("head")
    me = lax.axis_index("head").astype(jnp.int32)[None]
    start = doc_start[None, :] - lax.axis_index("ctx") * tok_rows + W
    steps = tok_rows // BLOCK

    def sent(block, distance):
        route = [(i, (i + distance) % pieces) for i in range(pieces)]
        return lax.ppermute(block, "head", route)

    def packed(head, after, *ends):
        return pack_call(
            head, me, out_cotangent, attn_output, kv_heads, groups * head_dim, pieces, after, *ends
        )

    def arrived(parts):
        return [part if k == 0 else sent(part, k) for k, part in enumerate(parts)]

    early = (kv_heads + 1) // 2
    *first, ends = packed(0, out_cotangent, (key_states, value_states), early)
    parts = {0: first}
    cotans = {0: arrived(first)}
    rims = [from_behind(ends, "ctx", 1)]
    after = first[0]
    for head in range(kv_heads - 1, 0, -1):
        parts[head] = packed(head, after)
        after = parts[head][0]
    if kv_heads > 1:
        held = lax.optimization_barrier((*parts[1], *cotans[0][1:]))
        parts[1], cotans[0][1:] = list(held[:pieces]), held[pieces:]
        cotans[1] = arrived(parts[1])
    if kv_heads > early:
        ends = rim_call(key_states, value_states, early, after)
        rims.append(from_behind(ends, "ctx", 1))

    split = 2 * W == tok_rows
    final = kv_heads - 1 if split else kv_heads
    before = []
    halos = None
    backs = []
    for head in range(kv_heads):
        later = parts[head + 2] if head + 2 < kv_heads else []
        halo = (head, final, halos) if head < final else (0, 1, None)
        call = functools.partial(
            head_call, head, me=me, queries=queries, rims=rims[int(head >= early)],
            rim_head=head - early * (head >= early), keys=key_states, values=value_states,
            lse=logsumexp, start=start, cotans=cotans[head], halo=halo,
        )
        if head + 1 < kv_heads or not split:
            got = call((0, steps), before=before, carry=[], passing=later[1:])
            if later:
                middle = pieces // 2
                moving = list(got[6:])
                held = lax.optimization_barrier((moving[middle - 1], *cotans[head + 1][1:]))
                moving[middle - 1] = held[0]
                cotans[head + 1][1:] = held[1:]
                cotans[head + 2] = arrived([later[0], *moving])
            before, halos = list(got[:5]), got[5]
        else:
            got = call((0, steps // 2), before=before[:1], carry=[], passing=[])
            halos = got[3]
        if head >= final - 1:
            backs.append(from_behind(halos, "ctx", -1))
        if head + 1 == kv_heads and split:
            before = call(
                (steps // 2, steps // 2), before=[got[0], *before[1:]], carry=got[1:3], passing=[]
            )
    grad_queries, grad_keys, grad_values, *tails = before
    grad_keys, grad_values = join_call(*tails, backs, grad_keys, grad_values)
    return grad_queries, grad_keys, grad_values


def solution(mesh):
    return jax.shard_map(
        body,
        mesh=mesh,
        in_specs=(
            P("head", "ctx", None),
            P("head", "ctx", None),
            P("head", "ctx", None),
            P(("ctx", "head"), None),
            P(("ctx", "head"), None),
            P("head", "ctx"),
            P("ctx"),
        ),
        out_specs=(P("head", "ctx", None), P("head", "ctx", None), P("head", "ctx", None)),
        check_vma=False,
    )
```
